128 devices in a mesh: section: 8 (over y_lo, x), peer: 16 (over y_hi, z, core).
Axes of the slice: x: 4, y: 4 (y_hi: 2, y_lo: 2; y = y_hi * 2 + y_lo), z: 4, core: 2. Of those that a mesh axis runs over, the one named last changes fastest.
Arguments:
- queries: bfloat16 [256, 16384], P(('section', 'peer')), may hold values from -256 to 256
- residual: bfloat16 [256, 16384], P(('section', 'peer')), may hold values from -3 to 3
- key_tile_store: bfloat16 [8, 256, 256, 1024], P('section', 'peer'), may hold values from -6 to 6
- value_tile_store: bfloat16 [8, 256, 256, 1024], P('section', 'peer'), may hold values from -6 to 6
- lengths: int32 [8, 32], P('section'), may hold values from 2 to 16384, as said below
- tile_request: int32 [8, 256], P('section', 'peer'), may hold values from 0 to 31, as said below
- tile_position: int32 [8, 256], P('section', 'peer'), may hold values from 0 to 63, as said below
Outputs:
- attended: bfloat16 [256, 16384], P(('section', 'peer'))
- next_hidden: bfloat16 [256, 16384], P(('section', 'peer'))
The draws below stay inside these ranges and needn't reach their ends.
Inputs may be any that keep to these rules, and one draw needn't show every extreme that they name: `tile_request`: every slot of a section is owned; each request of a section owns between 1 and 64 slots and exactly one request of each section owns 64; a request's slots lie in a run of consecutive slots, wrapping around the section's end. `tile_position`: the slots of a request hold its tile indices 0 to its slot count minus one, once each. `lengths`: A request owning c slots has a length above (c - 1) * 256 and at most c * 256; the request of each section that owns 64 slots has length 16384.
All inputs are finite; a program needn't handle non-finite values.
Results may differ from the reference program's by a relative error of at most 0.025.
Values may be sent and summed in bfloat16 or wider, within the bound.
A program may use at most 128 MiB of HBM per device.

```python
import jax
import jax.numpy as jnp
from jax import lax

D = 16384
QUERY_HEADS = 128
KEY_VALUE_HEADS = 8
HEAD_SIZE = 128
TILE_TOKENS = 256
R_SECTION = 32
SECTION_SLOTS = 256
MAX_TILES = 64
REQUESTS = 256
N_SECTION = 8


def section_plan(key):
    split_keys = jax.random.split(key, 4)
    others = R_SECTION - 1
    spare = SECTION_SLOTS - MAX_TILES - others
    even_share = spare // others
    leftover = spare % others
    ranks = jnp.arange(others, dtype=jnp.int32)
    counts = 1 + even_share + (ranks < leftover).astype(jnp.int32)
    half_count = others // 2
    shifted_units = jax.random.randint(split_keys[0], (half_count,), 0, even_share + 1).astype(jnp.int32)
    counts = counts.at[:half_count].add(-shifted_units)
    counts = counts.at[half_count:2 * half_count].add(shifted_units)
    counts = jnp.concatenate([jnp.full((1,), MAX_TILES, jnp.int32), counts])
    ordering = jax.random.permutation(split_keys[1], R_SECTION).astype(jnp.int32)
    run_ends = jnp.cumsum(counts).astype(jnp.int32)
    starts = run_ends - counts
    rotation = jax.random.randint(split_keys[2], (), 0, SECTION_SLOTS).astype(jnp.int32)
    physical = jnp.arange(SECTION_SLOTS, dtype=jnp.int32)
    logical = (physical - rotation) % SECTION_SLOTS
    runs = jnp.sum((run_ends[None, :] <= logical[:, None]).astype(jnp.int32), axis=1)
    owning_requests = ordering[runs]
    places = logical - starts[runs]
    tail_tokens = jax.random.randint(split_keys[3], (R_SECTION,), 2, TILE_TOKENS + 1).astype(jnp.int32)
    tail_tokens = jnp.where(counts == MAX_TILES, TILE_TOKENS, tail_tokens)
    run_lengths = (counts - 1) * TILE_TOKENS + tail_tokens
    lengths = jnp.zeros((R_SECTION,), jnp.int32).at[ordering].set(run_lengths)
    first_slots = jnp.zeros((R_SECTION,), jnp.int32).at[ordering].set((starts + rotation) % SECTION_SLOTS)
    return (owning_requests, places, lengths, first_slots)


def all_plans(key):
    sections = jnp.arange(N_SECTION, dtype=jnp.int32)

    def one_plan(section_index):
        return section_plan(jax.random.fold_in(key, section_index + 101))
    return jax.vmap(one_plan)(sections)


def key_tile(key, section_index, slot_index):
    tile_key_block = jax.random.fold_in(jax.random.fold_in(key, section_index + 7001), slot_index)
    return jnp.clip(jax.random.normal(tile_key_block, (TILE_TOKENS, KEY_VALUE_HEADS * HEAD_SIZE), jnp.float32), -6.0, 6.0)


def all_key_tiles(key):
    slot_ids = jnp.arange(SECTION_SLOTS, dtype=jnp.int32)

    def one_section(section_index):

        def one_slot(slot_index):
            return key_tile(key, section_index, slot_index)
        return jax.vmap(one_slot)(slot_ids)
    return jax.vmap(one_section)(jnp.arange(N_SECTION, dtype=jnp.int32))


def draw_key_tile_store(key, part):
    tiles = all_key_tiles(key)
    return tiles.astype(jnp.bfloat16)


def draw_queries(key, part):
    key = jax.random.fold_in(key, 5)
    token_row_block = N_SECTION * R_SECTION
    drawn = 2.5 * jax.random.normal(key, (token_row_block, QUERY_HEADS * HEAD_SIZE), jnp.float32)
    return jnp.clip(drawn, -256.0, 256.0).astype(jnp.bfloat16)


def draw_tile_request(key, part):
    plans = all_plans(key)
    return plans[0]


def draw_tile_position(key, part):
    plans = all_plans(key)
    return plans[1]


def draw_lengths(key, part):
    plans = all_plans(key)
    return plans[2]


def steps_of(stream_key, shape, cuts, low, largest):
    level, own = 1.0, jax.random.fold_in(stream_key, 6)
    for dim, shards_of in cuts:
        steps = jnp.exp(jax.random.uniform(jax.random.fold_in(own, dim), (shards_of,), jnp.float32, low / len(cuts), largest / len(cuts)))
        level = level * jnp.repeat(steps, shape[dim] // shards_of).reshape([-1 if axis == dim else 1 for axis in range(len(shape))])
    return level


def centred(stream_key, dims, width, most, cuts=(), kind=jnp.bfloat16):
    factor_of = steps_of(stream_key, dims, cuts, -0.22, 0.18) if cuts else 1.0
    array = jax.random.normal(stream_key, dims, jnp.float32) * width * factor_of
    return jnp.minimum(jnp.maximum(array, -most), most).astype(kind)


def setup_inputs(seed: int = 0) -> dict:
    keys = jax.random.split(jax.random.key(seed), 8)
    return {
        "queries": draw_queries(jax.random.fold_in(keys[7], 71), 0),
        "residual": centred(keys[1], (REQUESTS, D), 0.5, 3.0, ((0, 128),)),
        "key_tile_store": draw_key_tile_store(jax.random.fold_in(keys[7], 71), 0),
        "value_tile_store": centred(keys[3], (N_SECTION, SECTION_SLOTS, TILE_TOKENS, KEY_VALUE_HEADS * HEAD_SIZE), 1.0, 6.0, ((0, 8), (1, 16))),
        "lengths": draw_lengths(jax.random.fold_in(keys[7], 71), 0),
        "tile_request": draw_tile_request(jax.random.fold_in(keys[7], 71), 0),
        "tile_position": draw_tile_position(jax.random.fold_in(keys[7], 71), 0),
    }


def section_attend(inputs):
    query_section_rows, key_tile_stack, value_tile_stack, section_lengths, owning_requests, places = inputs
    query_group_width = QUERY_HEADS // KEY_VALUE_HEADS
    slot_total_count = key_tile_stack.shape[0]
    selected_slots = jnp.take(query_section_rows, owning_requests, axis=0).astype(jnp.float32).reshape(slot_total_count, KEY_VALUE_HEADS, query_group_width, HEAD_SIZE)
    key_head_spread = key_tile_stack.astype(jnp.float32).reshape(slot_total_count, TILE_TOKENS, KEY_VALUE_HEADS, HEAD_SIZE)
    scores = jnp.einsum("tgjd,tpgd->tgjp", selected_slots, key_head_spread) * (HEAD_SIZE ** -0.5)
    offsets = places[:, None] * TILE_TOKENS + jnp.arange(TILE_TOKENS, dtype=jnp.int32)[None, :]
    limits = jnp.take(section_lengths, owning_requests, axis=0)
    usable = offsets < limits[:, None]
    scores = jnp.where(usable[:, None, None, :], scores, -jnp.inf)
    tile_peak = jnp.max(scores, axis=3)
    member = owning_requests[None, :] == jnp.arange(R_SECTION, dtype=jnp.int32)[:, None]
    request_peak = jnp.max(jnp.where(member[:, :, None, None], tile_peak[None], -jnp.inf), axis=1)
    weights = jnp.exp(scores - jnp.take(request_peak, owning_requests, axis=0)[..., None]).astype(jnp.bfloat16)
    weight_wide = weights.astype(jnp.float32)
    totals = jnp.sum(weight_wide, axis=3)
    value_head_spread = value_tile_stack.astype(jnp.float32).reshape(slot_total_count, TILE_TOKENS, KEY_VALUE_HEADS, HEAD_SIZE)
    mixture = jnp.einsum("tgjp,tpgd->tgjd", weight_wide, value_head_spread)
    member_wide = member.astype(jnp.float32)
    request_total = jnp.einsum("rt,tgj->rgj", member_wide, totals, precision=lax.Precision.HIGHEST)
    request_mix = jnp.einsum("rt,tgjd->rgjd", member_wide, mixture, precision=lax.Precision.HIGHEST)
    return (request_mix / request_total[..., None]).reshape(R_SECTION, QUERY_HEADS * HEAD_SIZE).astype(jnp.bfloat16)


def reference(queries, residual, key_tile_store, value_tile_store, lengths, tile_request, tile_position):
    sectioned = queries.reshape(N_SECTION, R_SECTION, D)
    attended = lax.map(section_attend, (sectioned, key_tile_store, value_tile_store, lengths, tile_request, tile_position))
    attended = attended.reshape(N_SECTION * R_SECTION, D)
    held_rows = lax.optimization_barrier(attended)
    handed = (residual.astype(jnp.float32) + held_rows.astype(jnp.float32)).astype(jnp.bfloat16)
    next_hidden = jnp.roll(handed, R_SECTION, axis=0)
    return attended, next_hidden
```

```python
import functools

import jax
import jax.numpy as jnp
from jax import lax
from jax.experimental import pallas as pl
from jax.experimental.pallas import tpu as pltpu
from jax.sharding import PartitionSpec as P

PEERS = 16
SECTIONS = 8
SLOTS = 16
TILE = 256
HEADS = 128
HEAD = 128
REQUESTS = 32
PHASES = 4
PHASE_HEADS = HEADS // PHASES
GROUP = 16
UNROLL = 4
SCALE = HEAD ** (-0.5)
MESH = pl.DeviceIdType.MESH


def kernel(
    q_hbm, res_hbm, k_hbm, v_hbm, len_ref, req_ref, pos_ref,
    att_ref, nxt_ref, prev_res_ref,
    q_in, q_f32, q_send, gq0, gq1, gq2, gq3, kbuf, vbuf,
    x_f32, x_send, xr0, xr1, xr2, xr3,
    meta_f32, meta_send, mr0, mr1, mr2, mr3,
    fin_f32, fin_send,
    q_sem, kv_sem, gq_send_sem, gq_recv_sem, x_send_sem, x_recv_sem,
    m_send_sem, m_recv_sem, fin_send_sem, att_recv_sem, nxt_recv_sem, res_send_sem, res_recv_sem,
):
    gq = (gq0, gq1, gq2, gq3)
    xr = (xr0, xr1, xr2, xr3)
    mr = (mr0, mr1, mr2, mr3)
    me = lax.axis_index("peer")
    section = lax.axis_index("section")
    after = lax.rem(section + 1, SECTIONS)
    before = lax.rem(section + SECTIONS - 1, SECTIONS)

    q_copy = pltpu.make_async_copy(q_hbm, q_in, q_sem)
    q_copy.start()
    loads = []
    for p in range(PHASES):
        cols = pl.ds(p * 256, 256)
        for i, (src, dst) in enumerate(((k_hbm, kbuf), (v_hbm, vbuf))):
            load = pltpu.make_async_copy(
                src.at[0, :, :, cols], dst.at[p], kv_sem.at[p, i])
            load.start()
            loads.append(load)

    barrier = pltpu.get_barrier_semaphore()

    def greet_peer(d, carry):
        pl.semaphore_signal(
            barrier, inc=1, device_id=(section, lax.rem(me + d, PEERS)), device_id_type=MESH)
        return carry

    lax.fori_loop(1, PEERS, greet_peer, 0)

    def greet_before(d, carry):
        pl.semaphore_signal(
            barrier, inc=1, device_id=(before, d), device_id_type=MESH)
        return carry

    lax.fori_loop(0, PEERS, greet_before, 0)

    q_copy.wait()
    for h in range(HEADS):
        piece = q_in[:, h * HEAD:(h + 1) * HEAD].astype(jnp.float32)
        q_f32[0, h:h + 1, :] = piece[0:1]
        q_f32[1, h:h + 1, :] = piece[1:2]
    for p in range(PHASES):
        q_send[p] = q_f32[:, p * PHASE_HEADS:(p + 1) * PHASE_HEADS, :].astype(jnp.bfloat16)

    pl.semaphore_wait(barrier, 2 * PEERS - 1)

    for p in range(PHASES):
        def send_q(d, carry, p=p):
            pltpu.make_async_remote_copy(
                src_ref=q_send.at[p], dst_ref=gq[p].at[pl.ds(2 * me, 2)],
                send_sem=gq_send_sem, recv_sem=gq_recv_sem.at[p],
                device_id=(section, lax.rem(me + d, PEERS)), device_id_type=MESH).start()
            return carry

        pltpu.make_async_copy(
            q_send.at[p], gq[p].at[pl.ds(2 * me, 2)], gq_recv_sem.at[p]).start()
        lax.fori_loop(1, PEERS, send_q, 0)
    pass_residual = pltpu.make_async_remote_copy(
        src_ref=res_hbm, dst_ref=prev_res_ref, send_sem=res_send_sem, recv_sem=res_recv_sem,
        device_id=(after, me), device_id_type=MESH)
    pass_residual.start()

    token = lax.broadcasted_iota(jnp.int32, (PHASE_HEADS, TILE), 1)
    lane = lax.broadcasted_iota(jnp.int32, (PHASE_HEADS, 128), 1)
    zero_block = jnp.zeros((GROUP, HEAD), jnp.bfloat16)

    def merge(p):
        for ref, recv in ((xr[p], x_recv_sem.at[p]), (mr[p], m_recv_sem.at[p])):
            pltpu.make_async_copy(ref, ref, recv).wait()
        rows = jnp.concatenate([mr[p][e] for e in range(PEERS)], axis=0)
        lanes = lax.broadcasted_iota(jnp.int32, (8, 128), 1)
        own = lax.broadcasted_iota(jnp.int32, (8, 128), 0)
        mine = lanes // 16 == own

        def line(at):
            parts = []
            for half in (rows[0:8], rows[8:16]):
                if at:
                    half = pltpu.roll(half, 128 - at, 1)
                turned = pltpu.roll(half, 0, 1, stride=16, stride_axis=0)
                parts.append(jnp.sum(jnp.where(mine, turned, 0.0), axis=0, keepdims=True))
            return jnp.concatenate(parts, axis=1)

        order = lax.broadcasted_iota(jnp.int32, (REQUESTS, 2 * 128), 0)
        request = (2 * lax.rem(order, 16) + order // 16).astype(jnp.float32)
        for b in range(2):
            peak, total, code = line(64 * b), line(64 * b + 16), line(64 * b + 32)
            member = code == request
            held = jnp.where(member, peak, -jnp.inf)
            top = jnp.max(held, axis=1, keepdims=True)
            weight = jnp.exp(held - top).astype(jnp.bfloat16)
            whole = jnp.sum(weight.astype(jnp.float32) * total, axis=1, keepdims=True)
            mixed = jnp.dot(weight, xr[p][b], preferred_element_type=jnp.float32) / whole
            for i in range(2):
                fin_f32[pl.ds(2 * (2 * p + b) + i, 16, stride=16), :] = mixed[16 * i:16 * i + 16]

    for p in range(PHASES):
        pltpu.make_async_copy(gq[p], gq[p], gq_recv_sem.at[p]).wait()
        loads[2 * p].wait()
        loads[2 * p + 1].wait()

        def tiles(step, carry, p=p):
            peak, total, mix, meta = carry
            for u in range(UNROLL):
                t = step * UNROLL + u
                owner = req_ref[0, t]
                same = (t > 0) & (owner == req_ref[0, jnp.maximum(t - 1, 0)])
                closing = (t == SLOTS - 1) | (owner != req_ref[0, jnp.minimum(t + 1, SLOTS - 1)])
                code = jnp.where(closing, owner, -1).astype(jnp.float32)
                limit = len_ref[0, owner] - pos_ref[0, t] * TILE
                q = gq[p][owner]
                wide = jnp.concatenate(
                    [jnp.concatenate([q[:GROUP], zero_block], axis=1),
                     jnp.concatenate([zero_block, q[GROUP:]], axis=1)], axis=0)
                score = lax.dot_general(
                    wide, kbuf[p, t], (((1,), (1,)), ((), ())),
                    preferred_element_type=jnp.float32) * SCALE
                score = jnp.where(token < limit, score, -jnp.inf)
                old = jnp.where(same, peak, -jnp.inf)
                peak = jnp.maximum(old, jnp.max(score, axis=1, keepdims=True))
                keep = jnp.exp(old - peak)
                weight = jnp.exp(score - peak).astype(jnp.bfloat16)
                total = keep * total + jnp.sum(weight.astype(jnp.float32), axis=1, keepdims=True)
                both = jnp.dot(weight, vbuf[p, t], preferred_element_type=jnp.float32)
                mix = keep * mix + jnp.concatenate(
                    [both[:GROUP, :HEAD], both[GROUP:, HEAD:]], axis=0)
                x_f32[pl.ds(t, PHASE_HEADS, stride=SLOTS), :] = mix
                meta = jnp.where(lane == t, peak, meta)
                meta = jnp.where(lane == 16 + t, total, meta)
                meta = jnp.where(lane == 32 + t, code, meta)
            return peak, total, mix, meta

        _, _, _, meta = lax.fori_loop(
            0, SLOTS // UNROLL, tiles,
            (jnp.zeros((PHASE_HEADS, 1), jnp.float32), jnp.zeros((PHASE_HEADS, 1), jnp.float32),
             jnp.zeros((PHASE_HEADS, HEAD), jnp.float32), jnp.zeros((PHASE_HEADS, 128), jnp.float32)))
        x_send[p] = x_f32[...].astype(jnp.bfloat16).reshape(PEERS, 2, SLOTS, HEAD)
        meta_f32[...] = meta
        line = meta_f32[pl.ds(0, PEERS, stride=2), :] + pltpu.roll(
            meta_f32[pl.ds(1, PEERS, stride=2), :], 64, 1)
        for j in range(PEERS):
            meta_send[p, j] = line[j:j + 1]

        def send_x(d, carry, p=p):
            to = lax.rem(me + d, PEERS)
            pltpu.make_async_remote_copy(
                src_ref=x_send.at[p, to], dst_ref=xr[p].at[:, pl.ds(SLOTS * me, SLOTS), :],
                send_sem=x_send_sem, recv_sem=x_recv_sem.at[p],
                device_id=(section, to), device_id_type=MESH).start()
            pltpu.make_async_remote_copy(
                src_ref=meta_send.at[p, to], dst_ref=mr[p].at[me],
                send_sem=m_send_sem, recv_sem=m_recv_sem.at[p],
                device_id=(section, to), device_id_type=MESH).start()
            return carry

        pltpu.make_async_copy(
            x_send.at[p, me], xr[p].at[:, pl.ds(SLOTS * me, SLOTS), :], x_recv_sem.at[p]).start()
        pltpu.make_async_copy(
            meta_send.at[p, me], mr[p].at[me], m_recv_sem.at[p]).start()
        lax.fori_loop(1, PEERS, send_x, 0)
        if p > 0:
            merge(p - 1)
    merge(PHASES - 1)

    fin_send[...] = fin_f32[...].astype(jnp.bfloat16).reshape(PEERS, 16, HEAD)

    def send_home(d, carry):
        to = lax.rem(me + d, PEERS)
        pltpu.make_async_remote_copy(
            src_ref=fin_send.at[to], dst_ref=att_ref.at[me],
            send_sem=fin_send_sem, recv_sem=att_recv_sem,
            device_id=(section, to), device_id_type=MESH).start()
        return carry

    def send_after(d, carry):
        to = lax.rem(me + d, PEERS)
        pltpu.make_async_remote_copy(
            src_ref=fin_send.at[to], dst_ref=nxt_ref.at[me],
            send_sem=fin_send_sem, recv_sem=nxt_recv_sem,
            device_id=(after, to), device_id_type=MESH).start()
        return carry

    lax.fori_loop(0, PEERS, send_after, 0)
    pltpu.make_async_copy(fin_send.at[me], att_ref.at[me], att_recv_sem).start()
    lax.fori_loop(1, PEERS, send_home, 0)

    for p in range(PHASES):
        pltpu.make_async_copy(
            gq[p].at[pl.ds(0, 30)], gq[p].at[pl.ds(0, 30)], gq_send_sem).wait()
        pltpu.make_async_copy(
            x_send.at[p, pl.ds(0, 15)], x_send.at[p, pl.ds(0, 15)], x_send_sem).wait()
        pltpu.make_async_copy(
            meta_send.at[p, pl.ds(0, 15)], meta_send.at[p, pl.ds(0, 15)], m_send_sem).wait()
    pass_residual.wait()
    pltpu.make_async_copy(fin_send, fin_send, fin_send_sem).wait()
    pltpu.make_async_copy(
        fin_send.at[pl.ds(0, 15)], fin_send.at[pl.ds(0, 15)], fin_send_sem).wait()
    pltpu.make_async_copy(att_ref, att_ref, att_recv_sem).wait()
    pltpu.make_async_copy(nxt_ref, nxt_ref, nxt_recv_sem).wait()


def local(
    queries, residual, key_tile_store, value_tile_store, lengths, tile_request, tile_position
):
    any_spec = pl.BlockSpec(memory_space=pl.ANY)
    smem_spec = pl.BlockSpec(memory_space=pltpu.SMEM)
    vmem_spec = pl.BlockSpec(memory_space=pltpu.VMEM)
    dma = pltpu.SemaphoreType.DMA
    bf16, f32 = jnp.bfloat16, jnp.float32
    scratch = (
        [pltpu.VMEM((2, HEADS * HEAD), bf16), pltpu.VMEM((2, HEADS, HEAD), f32),
         pltpu.VMEM((PHASES, 2, PHASE_HEADS, HEAD), bf16)]
        + [pltpu.VMEM((REQUESTS, PHASE_HEADS, HEAD), bf16)] * PHASES
        + [pltpu.VMEM((PHASES, SLOTS, TILE, 256), bf16)] * 2
        + [pltpu.VMEM((PHASE_HEADS * SLOTS, HEAD), f32),
           pltpu.VMEM((PHASES, PEERS, 2, SLOTS, HEAD), bf16)]
        + [pltpu.VMEM((2, PEERS * SLOTS, HEAD), bf16)] * PHASES
        + [pltpu.VMEM((PHASE_HEADS, 128), f32), pltpu.VMEM((PHASES, PEERS, 1, 128), f32)]
        + [pltpu.VMEM((PEERS, 1, 128), f32)] * PHASES
        + [pltpu.VMEM((PEERS * 16, HEAD), f32), pltpu.VMEM((PEERS, 16, HEAD), bf16)]
        + [dma, dma((PHASES, 2)), dma, dma((PHASES,)), dma, dma((PHASES,)), dma, dma((PHASES,)),
           dma, dma, dma, dma, dma]
    )
    att, nxt, prev_res = pl.pallas_call(
        kernel,
        out_shape=(
            jax.ShapeDtypeStruct((PEERS, 16, HEAD), bf16),
            jax.ShapeDtypeStruct((PEERS, 16, HEAD), bf16),
            jax.ShapeDtypeStruct(residual.shape, bf16),
        ),
        in_specs=[any_spec] * 4 + [smem_spec] * 3,
        out_specs=[vmem_spec, vmem_spec, vmem_spec],
        scratch_shapes=scratch,
        compiler_params=pltpu.CompilerParams(
            collective_id=0, has_side_effects=True, vmem_limit_bytes=60 * 1024 * 1024),
    )(queries, residual, key_tile_store, value_tile_store, lengths, tile_request, tile_position)

    def home(block):
        block = block.reshape(PEERS, PHASES, 2, 2, HEAD)
        return block.transpose(3, 1, 0, 2, 4).reshape(2, HEADS * HEAD)

    attended = home(att)
    next_hidden = (prev_res.astype(f32) + home(nxt).astype(f32)).astype(bf16)
    return attended, next_hidden


def solution(mesh):
    in_specs = (
        P(("section", "peer"), None),
        P(("section", "peer"), None),
        P("section", "peer", None, None),
        P("section", "peer", None, None),
        P("section", None),
        P("section", "peer"),
        P("section", "peer"),
    )
    out_specs = (P(("section", "peer"), None), P(("section", "peer"), None))
    return jax.shard_map(local, mesh=mesh, in_specs=in_specs, out_specs=out_specs, check_vma=False)
```

```python
import jax
import jax.numpy as jnp
from jax import lax
from jax.experimental import pallas as pl
from jax.experimental.pallas import tpu as pltpu
from jax.sharding import PartitionSpec as P

PEERS = 16
CHIPS = 8
SECTIONS = 8
SLOTS = 16
TILE = 256
HEADS = 128
HEAD = 128
REQUESTS = 32
PHASES = 4
PHASE_HEADS = HEADS // PHASES
GROUP = 16
SCALE = HEAD ** (-0.5)
MESH = pl.DeviceIdType.MESH


def landed(ref, sem):
    pltpu.make_async_copy(ref, ref, sem).wait()


def kernel(
    q_hbm, res_hbm, k_hbm, v_hbm, len_ref, req_ref, pos_ref,
    att_ref, nxt_ref,
    q_in, res_in, q_f32, res_f32, q_send, gq0, gq1, gq2, gq3, kbuf, vbuf,
    scores, weights, sums_of, place, meta_own, twin_send, twin_x0, twin_x1, twin_x2, twin_x3, twin_meta,
    x_send, xr0, xr1, xr2, xr3, m_send, mr0, mr1, mr2, mr3, hand_send,
    q_sem, res_sem, kv_sem, gq_send_sem, gq_recv_sem, gq_twin_sem,
    twin_x_send_sem, twin_x_sem, twin_m_send_sem, twin_m_sem,
    x_send_sem, x_sem, m_send_sem, m_sem, hand_send_sem, hand_sem,
):
    gq = (gq0, gq1, gq2, gq3)
    twin_x = (twin_x0, twin_x1, twin_x2, twin_x3)
    xr = (xr0, xr1, xr2, xr3)
    mr = (mr0, mr1, mr2, mr3)
    me = lax.axis_index("peer")
    section = lax.axis_index("section")
    core, chip = lax.rem(me, 2), me // 2
    twin = me + 1 - 2 * core
    after = lax.rem(section + 1, SECTIONS)
    before = lax.rem(section + SECTIONS - 1, SECTIONS)

    barrier = pltpu.get_barrier_semaphore()

    def greet(d, carry):
        pl.semaphore_signal(
            barrier, inc=1, device_id=(section, lax.rem(me + 2 * d, PEERS)), device_id_type=MESH)
        return carry

    lax.fori_loop(1, CHIPS, greet, 0)
    pl.semaphore_signal(barrier, inc=1, device_id=(before, me), device_id_type=MESH)
    pl.semaphore_signal(barrier, inc=1, device_id=(section, twin), device_id_type=MESH)

    q_copy = pltpu.make_async_copy(q_hbm, q_in, q_sem)
    q_copy.start()
    res_copy = pltpu.make_async_copy(res_hbm, res_in, res_sem)
    res_copy.start()
    loads = []
    for p in range(PHASES):
        cols = pl.ds(p * 256, 256)
        for i, (src, dst) in enumerate(((k_hbm, kbuf), (v_hbm, vbuf))):
            load = pltpu.make_async_copy(
                src.at[0, :, :, cols], dst.at[p], kv_sem.at[p, i])
            load.start()
            loads.append(load)

    def spread(rows, out):
        for h in range(HEADS):
            piece = rows[:, h * HEAD:(h + 1) * HEAD].astype(jnp.float32)
            out[0, h:h + 1, :] = piece[0:1]
            out[1, h:h + 1, :] = piece[1:2]

    q_copy.wait()
    spread(q_in, q_f32)
    for p in range(PHASES):
        q_send[p] = q_f32[:, p * PHASE_HEADS:(p + 1) * PHASE_HEADS, :].astype(jnp.bfloat16)

    pl.semaphore_wait(barrier, CHIPS + 1)

    for p in range(PHASES):
        def send_q(d, carry, p=p):
            pltpu.make_async_remote_copy(
                src_ref=q_send.at[p], dst_ref=gq[p].at[core, chip],
                send_sem=gq_send_sem, recv_sem=gq_recv_sem.at[p],
                device_id=(section, lax.rem(me + 2 * d, PEERS)), device_id_type=MESH).start()
            return carry

        pltpu.make_async_copy(q_send.at[p], gq[p].at[core, chip], gq_recv_sem.at[p]).start()
        lax.fori_loop(1, CHIPS, send_q, 0)

    def pass_queries(p):
        landed(gq[p].at[core], gq_recv_sem.at[p])
        copy = pltpu.make_async_remote_copy(
            src_ref=gq[p].at[core], dst_ref=gq[p].at[core],
            send_sem=gq_send_sem, recv_sem=gq_twin_sem.at[p],
            device_id=(section, twin), device_id_type=MESH)
        copy.start()
        return copy

    res_copy.wait()
    spread(res_in, res_f32)

    token = lax.broadcasted_iota(jnp.int32, (PHASE_HEADS, TILE), 1)
    lane = lax.broadcasted_iota(jnp.int32, (PHASE_HEADS, 128), 1)
    zero_block = jnp.zeros((GROUP, HEAD), jnp.bfloat16)
    ones = jnp.ones((TILE, HEAD), jnp.bfloat16)
    owner = [req_ref[0, t] for t in range(SLOTS)]
    limit = [len_ref[0, owner[t]] - pos_ref[0, t] * TILE for t in range(SLOTS)]
    same = [owner[t] == owner[t - 1] for t in range(1, SLOTS)]
    last = [jnp.where(same[t], -1, owner[t]) for t in range(SLOTS - 1)] + [owner[SLOTS - 1]]
    for r in range(REQUESTS):
        at = jnp.int32(0)
        for t in range(SLOTS):
            at = jnp.where(last[t] == r, t, at)
        place[r] = at
    column = [
        jnp.where(r < 0, -128, ((r >> 1) & 1) * 64 + (r >> 2) * 4 + (r & 1)) for r in last]
    is_peak = (lane & 3) < 2

    def attend(p):
        tops = []
        for t in range(SLOTS):
            r = owner[t]
            q = gq[p][(r >> 1) & 1, r >> 2, r & 1]
            wide = jnp.concatenate(
                [jnp.concatenate([q[:GROUP], zero_block], axis=1),
                 jnp.concatenate([zero_block, q[GROUP:]], axis=1)], axis=0)
            score = lax.dot_general(
                wide, kbuf[p, t], (((1,), (1,)), ((), ())),
                preferred_element_type=jnp.float32) * SCALE
            score = jnp.where(token < limit[t], score, -jnp.inf)
            scores[t] = score
            tops.append(jnp.max(
                jnp.maximum(score[:, :128], score[:, 128:]), axis=1, keepdims=True))
        for t in range(1, SLOTS):
            tops[t] = jnp.maximum(jnp.where(same[t - 1], tops[t - 1], -jnp.inf), tops[t])
        for t in range(SLOTS - 2, -1, -1):
            tops[t] = jnp.where(same[t], tops[t + 1], tops[t])
        mix = None
        for t in range(SLOTS):
            weight = jnp.exp(scores[t] - tops[t]).astype(jnp.bfloat16)
            weights[pl.ds(PHASE_HEADS * t, PHASE_HEADS), :] = weight
            both = jnp.dot(weight, vbuf[p, t], preferred_element_type=jnp.float32)
            part = jnp.concatenate([both[:GROUP, :HEAD], both[GROUP:, HEAD:]], axis=0)
            mix = part if t == 0 else jnp.where(same[t - 1], mix, 0.0) + part
            sums_of[p, t] = mix
        sums = jnp.dot(weights[...], ones, preferred_element_type=jnp.float32)
        meta = jnp.where(is_peak, -jnp.inf, 0.0)
        total = None
        for t in range(SLOTS):
            part = sums[PHASE_HEADS * t:PHASE_HEADS * (t + 1)]
            total = part if t == 0 else jnp.where(same[t - 1], total, 0.0) + part
            meta = jnp.where(lane == column[t], tops[t], meta)
            meta = jnp.where(lane == column[t] + 2, total, meta)
        meta_own[p] = meta
        pltpu.make_async_remote_copy(
            src_ref=meta_own.at[p], dst_ref=twin_meta.at[p],
            send_sem=twin_m_send_sem, recv_sem=twin_m_sem.at[p],
            device_id=(section, twin), device_id_type=MESH).start()
        for c in range(CHIPS):
            for i in range(2):
                twin_send[p, c, i] = sums_of[p, place[4 * c + 2 * (1 - core) + i]].astype(jnp.bfloat16)
        pltpu.make_async_remote_copy(
            src_ref=twin_send.at[p], dst_ref=twin_x[p],
            send_sem=twin_x_send_sem, recv_sem=twin_x_sem.at[p],
            device_id=(section, twin), device_id_type=MESH).start()

    def join_cores(p):
        landed(meta_own.at[p], twin_m_sem.at[p])
        here = pltpu.roll(meta_own[p], 64 * core, 1)
        there = pltpu.roll(twin_meta[p], 64 * core, 1)
        peak = jnp.maximum(here, there)
        base = jnp.where(peak == -jnp.inf, 0.0, peak)
        used = is_peak & (lane < 32)
        by_here = jnp.where(used, jnp.exp(here - base), 0.0)
        by_there = jnp.where(used, jnp.exp(there - base), 0.0)
        total = by_here * pltpu.roll(here, 126, 1) + by_there * pltpu.roll(there, 126, 1)
        total = jnp.where(used, total, 0.0)
        meta = jnp.where(is_peak, peak, pltpu.roll(total, 2, 1))
        turned = jnp.concatenate(
            [meta, jnp.zeros((128 - PHASE_HEADS, 128), jnp.float32)], axis=0).T
        for c in range(CHIPS):
            m_send[p, c] = turned[4 * c:4 * c + 4]
        landed(twin_x[p], twin_x_sem.at[p])
        for c in range(CHIPS):
            for i in range(2):
                at = 4 * c + i
                own = sums_of[p, place[4 * c + 2 * core + i]]
                other = twin_x[p][c, i].astype(jnp.float32)
                x_send[p, c, i] = (
                    by_here[:, at:at + 1] * own + by_there[:, at:at + 1] * other).astype(jnp.bfloat16)

        def send_x(d, carry):
            to = lax.rem(chip + d, CHIPS)
            pltpu.make_async_remote_copy(
                src_ref=x_send.at[p, to], dst_ref=xr[p].at[chip],
                send_sem=x_send_sem, recv_sem=x_sem.at[p],
                device_id=(section, 2 * to + core), device_id_type=MESH).start()
            pltpu.make_async_remote_copy(
                src_ref=m_send.at[p, to], dst_ref=mr[p].at[chip],
                send_sem=m_send_sem, recv_sem=m_sem.at[p],
                device_id=(section, 2 * to + core), device_id_type=MESH).start()
            return carry

        lax.fori_loop(1, CHIPS, send_x, 0)
        pltpu.make_async_copy(x_send.at[p, chip], xr[p].at[chip], x_sem.at[p]).start()
        pltpu.make_async_copy(m_send.at[p, chip], mr[p].at[chip], m_sem.at[p]).start()

    def join_chips(p):
        landed(mr[p], m_sem.at[p])
        rows = jnp.concatenate([mr[p][c] for c in range(CHIPS)], axis=0)
        meta = jnp.concatenate(
            [rows, jnp.zeros((128 - 4 * CHIPS, 128), jnp.float32)], axis=0).T[:PHASE_HEADS]
        totals = pltpu.roll(meta, 126, 1)
        landed(xr[p], x_sem.at[p])
        heads = pl.ds(p * PHASE_HEADS, PHASE_HEADS)
        for i in range(2):
            used = ((lane & 3) == i) & (lane < 4 * CHIPS)
            peaks = jnp.where(used, meta, -jnp.inf)
            part = jnp.exp(peaks - jnp.max(peaks, axis=1, keepdims=True))
            whole = jnp.sum(jnp.where(used, part * totals, 0.0), axis=1, keepdims=True)
            part = part / whole
            mix = None
            for c in range(CHIPS):
                at = 4 * c + i
                term = part[:, at:at + 1] * xr[p][c, i].astype(jnp.float32)
                mix = term if mix is None else mix + term
            attended = mix.astype(jnp.bfloat16)
            att_ref[i, heads, :] = attended
            hand_send[p, i] = (
                res_f32[i, heads, :] + attended.astype(jnp.float32)).astype(jnp.bfloat16)
        pltpu.make_async_remote_copy(
            src_ref=hand_send.at[p], dst_ref=nxt_ref.at[:, heads, :],
            send_sem=hand_send_sem, recv_sem=hand_sem,
            device_id=(after, me), device_id_type=MESH).start()

    passed = [pass_queries(0), pass_queries(1)]
    for p in range(PHASES):
        passed[p].wait_recv()
        loads[2 * p].wait()
        loads[2 * p + 1].wait()
        attend(p)
        if p + 2 < PHASES:
            passed.append(pass_queries(p + 2))
        if p > 0:
            join_cores(p - 1)
    join_cores(PHASES - 1)
    for p in range(PHASES):
        join_chips(p)

    for p in range(PHASES):
        landed(gq[p].at[0, pl.ds(0, 7)], gq_send_sem)
        landed(gq[p].at[0], gq_send_sem)
        landed(x_send.at[p, pl.ds(0, 7)], x_send_sem)
        landed(m_send.at[p, pl.ds(0, 7)], m_send_sem)
    landed(twin_send, twin_x_send_sem)
    landed(meta_own, twin_m_send_sem)
    landed(hand_send, hand_send_sem)
    landed(nxt_ref, hand_sem)


def local(
    queries, residual, key_tile_store, value_tile_store, lengths, tile_request, tile_position
):
    any_spec = pl.BlockSpec(memory_space=pl.ANY)
    smem_spec = pl.BlockSpec(memory_space=pltpu.SMEM)
    vmem_spec = pl.BlockSpec(memory_space=pltpu.VMEM)
    dma = pltpu.SemaphoreType.DMA
    bf16, f32 = jnp.bfloat16, jnp.float32
    scratch = (
        [pltpu.VMEM((2, HEADS * HEAD), bf16)] * 2
        + [pltpu.VMEM((2, HEADS, HEAD), f32)] * 2
        + [pltpu.VMEM((PHASES, 2, PHASE_HEADS, HEAD), bf16)]
        + [pltpu.VMEM((2, CHIPS, 2, PHASE_HEADS, HEAD), bf16)] * PHASES
        + [pltpu.VMEM((PHASES, SLOTS, TILE, 256), bf16)] * 2
        + [pltpu.VMEM((SLOTS, PHASE_HEADS, TILE), f32), pltpu.VMEM((SLOTS * PHASE_HEADS, TILE), bf16),
           pltpu.VMEM((PHASES, SLOTS, PHASE_HEADS, HEAD), f32), pltpu.SMEM((REQUESTS,), jnp.int32),
           pltpu.VMEM((PHASES, PHASE_HEADS, 128), f32),
           pltpu.VMEM((PHASES, CHIPS, 2, PHASE_HEADS, HEAD), bf16)]
        + [pltpu.VMEM((CHIPS, 2, PHASE_HEADS, HEAD), bf16)] * PHASES
        + [pltpu.VMEM((PHASES, PHASE_HEADS, 128), f32),
           pltpu.VMEM((PHASES, CHIPS, 2, PHASE_HEADS, HEAD), bf16)]
        + [pltpu.VMEM((CHIPS, 2, PHASE_HEADS, HEAD), bf16)] * PHASES
        + [pltpu.VMEM((PHASES, CHIPS, 4, 128), f32)]
        + [pltpu.VMEM((CHIPS, 4, 128), f32)] * PHASES
        + [pltpu.VMEM((PHASES, 2, PHASE_HEADS, HEAD), bf16)]
        + [dma, dma, dma((PHASES, 2)), dma, dma((PHASES,)), dma((PHASES,)),
           dma, dma((PHASES,)), dma, dma((PHASES,)), dma, dma((PHASES,)), dma, dma((PHASES,)), dma, dma]
    )
    attended, handed = pl.pallas_call(
        kernel,
        out_shape=(jax.ShapeDtypeStruct((2, HEADS, HEAD), bf16),) * 2,
        in_specs=[any_spec] * 4 + [smem_spec] * 3,
        out_specs=[vmem_spec] * 2,
        scratch_shapes=scratch,
        compiler_params=pltpu.CompilerParams(
            collective_id=0, has_side_effects=True, vmem_limit_bytes=60 * 1024 * 1024),
    )(queries, residual, key_tile_store, value_tile_store, lengths, tile_request, tile_position)
    return attended.reshape(queries.shape), handed.reshape(queries.shape)


def solution(mesh):
    in_specs = (
        P(("section", "peer"), None),
        P(("section", "peer"), None),
        P("section", "peer", None, None),
        P("section", "peer", None, None),
        P("section", None),
        P("section", "peer"),
        P("section", "peer"),
    )
    out_specs = (P(("section", "peer"), None), P(("section", "peer"), None))
    return jax.shard_map(local, mesh=mesh, in_specs=in_specs, out_specs=out_specs, check_vma=False)
```

```python
import jax
import jax.numpy as jnp
from jax import lax
from jax.experimental import pallas as pl
from jax.experimental.pallas import tpu as pltpu
from jax.sharding import PartitionSpec as P

PEERS = 16
CHIPS = 8
SECTIONS = 8
SLOTS = 16
TILE = 256
HEADS = 128
HEAD = 128
REQUESTS = 32
GROUP = 16
WIDTHS = (2, 2, 2, 2)
PHASES = len(WIDTHS)
FIRST = [sum(WIDTHS[:p]) for p in range(PHASES)]
ROWS = [GROUP * w for w in WIDTHS]
SCALE = HEAD ** (-0.5)
NONE = -1e30
STEPS = ((1, 2), (1, 1), (1, 3), (1, 0), (0, 2), (0, 1), (0, 3))
WIDE = [-(-4 * r // 128) for r in ROWS]
BLOCKS = [2 * r + 16 for r in ROWS]
MESH = pl.DeviceIdType.MESH


def widen(block):
    rest = 128 - block.shape[1]
    if not rest:
        return block
    return jnp.concatenate([block, jnp.zeros((block.shape[0], rest), block.dtype)], axis=1)


def landed(ref, sem):
    pltpu.make_async_copy(ref, ref, sem).wait()


def kernel(
    q_hbm, res_hbm, k_hbm, v_hbm, len_hbm, req_hbm, pos_hbm,
    att_ref, nxt_ref,
    len_ref, req_ref, pos_ref, q_in, res_in, q_f32, res_f32, place, *rest,
):
    q_send, gq, kbuf, vbuf, scores, sums_of, meta_own, twin_meta, twin_send, twin_x, x_send, xr, hand_send = (
        rest[i * PHASES:(i + 1) * PHASES] for i in range(13))
    (
        q_sem, res_sem, plan_sem, kv_sem, gq_send_sem, gq_recv_sem, gq_twin_sem,
        twin_x_send_sem, twin_x_sem, twin_m_send_sem, twin_m_sem,
        x_send_sem, x_sem, hand_send_sem, hand_sem,
    ) = rest[13 * PHASES:]
    me = lax.axis_index("peer")
    section = lax.axis_index("section")
    core, chip = lax.rem(me, 2), me // 2
    y, z = chip // 4, lax.rem(chip, 4)
    others = [lax.rem(y + dy, 2) * 4 + lax.rem(z + dz, 4) for dy, dz in STEPS]
    twin = me + 1 - 2 * core
    after = lax.rem(section + 1, SECTIONS)
    before = lax.rem(section + SECTIONS - 1, SECTIONS)

    barrier = pltpu.get_barrier_semaphore()

    for to in others:
        pl.semaphore_signal(
            barrier, inc=1, device_id=(section, 2 * to + core), device_id_type=MESH)
    pl.semaphore_signal(barrier, inc=1, device_id=(before, me), device_id_type=MESH)
    pl.semaphore_signal(barrier, inc=1, device_id=(section, twin), device_id_type=MESH)

    q_copy = pltpu.make_async_copy(q_hbm, q_in, q_sem)
    q_copy.start()
    res_copy = pltpu.make_async_copy(res_hbm, res_in, res_sem)
    res_copy.start()
    plan = []
    for i, (src, dst) in enumerate(((len_hbm, len_ref), (req_hbm, req_ref), (pos_hbm, pos_ref))):
        plan.append(pltpu.make_async_copy(src, dst, plan_sem.at[i]))
        plan[i].start()
    def spread(rows, out):
        for h in range(HEADS):
            piece = rows[:, h * HEAD:(h + 1) * HEAD].astype(jnp.float32)
            out[0, h:h + 1, :] = piece[0:1]
            out[1, h:h + 1, :] = piece[1:2]

    q_copy.wait()
    spread(q_in, q_f32)
    for p in range(PHASES):
        q_send[p][...] = q_f32[:, GROUP * FIRST[p]:GROUP * FIRST[p] + ROWS[p], :].astype(jnp.bfloat16)

    pl.semaphore_wait(barrier, CHIPS + 1)

    for p in range(PHASES):
        for to in others:
            pltpu.make_async_remote_copy(
                src_ref=q_send[p], dst_ref=gq[p].at[core, chip],
                send_sem=gq_send_sem.at[p], recv_sem=gq_recv_sem.at[p],
                device_id=(section, 2 * to + core), device_id_type=MESH).start()
        pltpu.make_async_copy(q_send[p], gq[p].at[core, chip], gq_recv_sem.at[p]).start()
    loads = []
    for p in range(PHASES):
        cols = pl.ds(FIRST[p] * HEAD, WIDTHS[p] * HEAD)
        for i, (src, dst) in enumerate(((k_hbm, kbuf), (v_hbm, vbuf))):
            load = pltpu.make_async_copy(
                src.at[0, :, :, cols], dst[p], kv_sem.at[p, i])
            load.start()
            loads.append(load)

    def pass_queries(p):
        landed(gq[p].at[core], gq_recv_sem.at[p])
        copy = pltpu.make_async_remote_copy(
            src_ref=gq[p].at[core], dst_ref=gq[p].at[core],
            send_sem=gq_send_sem.at[p], recv_sem=gq_twin_sem.at[p],
            device_id=(section, twin), device_id_type=MESH)
        copy.start()
        return copy

    res_copy.wait()
    spread(res_in, res_f32)
    for copy in plan:
        copy.wait()

    token = lax.broadcasted_iota(jnp.int32, (1, TILE), 1)
    owner = [req_ref[0, t] for t in range(SLOTS)]
    limit = [len_ref[0, owner[t]] - pos_ref[0, t] * TILE for t in range(SLOTS)]
    same = [owner[t] == owner[t - 1] for t in range(1, SLOTS)]
    last = [jnp.where(same[t], -1, owner[t]) for t in range(SLOTS - 1)] + [owner[SLOTS - 1]]
    for r in range(REQUESTS):
        at = jnp.int32(0)
        for t in range(SLOTS):
            at = jnp.where(last[t] == r, t, at)
        place[r] = at
    column = [
        jnp.where(r < 0, -128, ((r >> 1) & 1) * 64 + (r & 1) * 8 + (r >> 2)) for r in last]

    def lanes(p):
        return lax.broadcasted_iota(jnp.int32, (ROWS[p], 128), 1)

    def attend(p):
        lane = lanes(p)
        tops = []
        for t in range(SLOTS):
            r = owner[t]
            q = gq[p][(r >> 1) & 1, r >> 2, r & 1]
            score = jnp.concatenate(
                [lax.dot_general(
                    q[GROUP * g:GROUP * (g + 1)], kbuf[p][t, :, HEAD * g:HEAD * (g + 1)],
                    (((1,), (1,)), ((), ())), preferred_element_type=jnp.float32)
                 for g in range(WIDTHS[p])], axis=0) * SCALE
            score = jnp.where(token < limit[t], score, -jnp.inf)
            scores[p][t] = score
            tops.append(jnp.max(
                jnp.maximum(score[:, :128], score[:, 128:]), axis=1, keepdims=True))
        for t in range(1, SLOTS):
            tops[t] = jnp.maximum(jnp.where(same[t - 1], tops[t - 1], -jnp.inf), tops[t])
        for t in range(SLOTS - 2, -1, -1):
            tops[t] = jnp.where(same[t], tops[t + 1], tops[t])
        mix, total = None, None
        meta = jnp.where((lane & 63) < 16, NONE, 0.0)
        for t in range(SLOTS):
            weight = jnp.exp(scores[p][t] - tops[t]).astype(jnp.bfloat16)
            part = jnp.concatenate(
                [jnp.dot(
                    weight[GROUP * g:GROUP * (g + 1)], vbuf[p][t, :, HEAD * g:HEAD * (g + 1)],
                    preferred_element_type=jnp.float32)
                 for g in range(WIDTHS[p])], axis=0)
            wide = weight.astype(jnp.float32)
            count = jnp.sum(wide[:, :128] + wide[:, 128:], axis=1, keepdims=True)
            mix = part if t == 0 else jnp.where(same[t - 1], mix, 0.0) + part
            total = count if t == 0 else jnp.where(same[t - 1], total, 0.0) + count
            sums_of[p][t] = mix
            meta = jnp.where(lane == column[t], tops[t], meta)
            meta = jnp.where(lane == column[t] + 16, total, meta)
        meta_own[p][...] = meta
        pltpu.make_async_remote_copy(
            src_ref=meta_own[p], dst_ref=twin_meta[p],
            send_sem=twin_m_send_sem.at[p], recv_sem=twin_m_sem.at[p],
            device_id=(section, twin), device_id_type=MESH).start()
        for c in range(CHIPS):
            for i in range(2):
                twin_send[p][c, i] = sums_of[p][place[4 * c + 2 * (1 - core) + i]].astype(jnp.bfloat16)
        pltpu.make_async_remote_copy(
            src_ref=twin_send[p], dst_ref=twin_x[p],
            send_sem=twin_x_send_sem.at[p], recv_sem=twin_x_sem.at[p],
            device_id=(section, twin), device_id_type=MESH).start()

    def join_cores(p):
        lane, rows = lanes(p), ROWS[p]
        landed(twin_meta[p], twin_m_sem.at[p])
        here = pltpu.roll(meta_own[p][...], 64 * core, 1)
        there = pltpu.roll(twin_meta[p][...], 64 * core, 1)
        peak = jnp.maximum(here, there)
        by_here, by_there = jnp.exp(here - peak), jnp.exp(there - peak)
        total = by_here * pltpu.roll(here, 112, 1) + by_there * pltpu.roll(there, 112, 1)
        meta = jnp.where(lane < 16, peak, jnp.where(lane < 32, pltpu.roll(total, 16, 1), 0.0))
        turned = jnp.concatenate([meta, jnp.zeros((128 - rows, 128), jnp.float32)], axis=0).T
        kinds = [turned[CHIPS * i:CHIPS * (i + 1), :rows] for i in range(4)]
        per = 4 // WIDE[p]
        lines = [
            widen(jnp.concatenate(kinds[per * j:per * (j + 1)], axis=1)) for j in range(WIDE[p])]
        split = []
        for line in lines:
            high = line.astype(jnp.bfloat16).astype(jnp.float32)
            middle = (line - high).astype(jnp.bfloat16).astype(jnp.float32)
            split += [high, middle, line - high - middle]
        for c in range(CHIPS):
            x_send[p][c, 2 * rows:, :] = jnp.concatenate(
                [part[c:c + 1] for part in split]
                + [jnp.zeros((16 - len(split), 128), jnp.float32)], axis=0).astype(jnp.bfloat16)
        landed(twin_x[p], twin_x_sem.at[p])
        for c in range(CHIPS):
            for i in range(2):
                at = 8 * i + c
                own = sums_of[p][place[4 * c + 2 * core + i]]
                other = twin_x[p][c, i].astype(jnp.float32)
                x_send[p][c, rows * i:rows * (i + 1), :] = (
                    by_here[:, at:at + 1] * own + by_there[:, at:at + 1] * other).astype(jnp.bfloat16)
        for to in others:
            pltpu.make_async_remote_copy(
                src_ref=x_send[p].at[to], dst_ref=xr[p].at[chip],
                send_sem=x_send_sem.at[p], recv_sem=x_sem.at[p],
                device_id=(section, 2 * to + core), device_id_type=MESH).start()
        pltpu.make_async_copy(x_send[p].at[chip], xr[p].at[chip], x_sem.at[p]).start()

    def join_chips(p):
        lane, rows, got = lanes(p), ROWS[p], xr[p]
        landed(got, x_sem.at[p])
        heads = pl.ds(GROUP * FIRST[p], rows)
        per = 4 // WIDE[p]
        lines = [[] for _ in range(WIDE[p])]
        for c in range(CHIPS):
            tile = got[c, 2 * rows:, :].astype(jnp.float32)
            for j in range(WIDE[p]):
                lines[j].append(tile[3 * j:3 * j + 1] + tile[3 * j + 1:3 * j + 2] + tile[3 * j + 2:3 * j + 3])
        lines = [jnp.concatenate(line, axis=0) for line in lines]
        kinds = jnp.concatenate(
            [lines[i // per][:, rows * (i % per):rows * (i % per + 1)] for i in range(4)], axis=0)
        meta = jnp.concatenate([widen(kinds), jnp.zeros((128 - 32, 128), jnp.float32)], axis=0).T[:rows]
        totals = pltpu.roll(meta, 112, 1)
        for i in range(2):
            used = (lane >> 3) == i
            peaks = jnp.where(used, meta, NONE)
            part = jnp.exp(peaks - jnp.max(peaks, axis=1, keepdims=True))
            whole = jnp.sum(jnp.where(used, part * totals, 0.0), axis=1, keepdims=True)
            part = part / whole
            mix = None
            for c in range(CHIPS):
                at = 8 * i + c
                term = part[:, at:at + 1] * got[c, rows * i:rows * (i + 1), :].astype(jnp.float32)
                mix = term if mix is None else mix + term
            attended = mix.astype(jnp.bfloat16)
            att_ref[i, heads, :] = attended
            hand_send[p][i] = (
                res_f32[i, heads, :] + attended.astype(jnp.float32)).astype(jnp.bfloat16)
        pltpu.make_async_remote_copy(
            src_ref=hand_send[p], dst_ref=nxt_ref.at[:, heads, :],
            send_sem=hand_send_sem.at[p], recv_sem=hand_sem,
            device_id=(after, me), device_id_type=MESH).start()

    passed = [pass_queries(0), pass_queries(1)]
    for p in range(PHASES):
        passed[p].wait_recv()
        loads[2 * p].wait()
        loads[2 * p + 1].wait()
        attend(p)
        if p + 2 < PHASES:
            passed.append(pass_queries(p + 2))
        if p > 0:
            join_cores(p - 1)
    join_cores(PHASES - 1)
    for p in range(PHASES):
        join_chips(p)

    for p in range(PHASES):
        landed(gq[p].at[0, pl.ds(0, 7)], gq_send_sem.at[p])
        landed(gq[p].at[0], gq_send_sem.at[p])
        landed(x_send[p].at[pl.ds(0, 7)], x_send_sem.at[p])
        landed(twin_send[p], twin_x_send_sem.at[p])
        landed(meta_own[p], twin_m_send_sem.at[p])
        landed(hand_send[p], hand_send_sem.at[p])
    landed(nxt_ref, hand_sem)


def local(
    queries, residual, key_tile_store, value_tile_store, lengths, tile_request, tile_position
):
    any_spec = pl.BlockSpec(memory_space=pl.ANY)
    vmem_spec = pl.BlockSpec(memory_space=pltpu.VMEM)
    dma = pltpu.SemaphoreType.DMA
    bf16, f32 = jnp.bfloat16, jnp.float32
    def each(dtype, shape):
        return [pltpu.VMEM(shape(w, r, n), dtype) for w, r, n in zip(WIDTHS, ROWS, BLOCKS, strict=True)]

    sums = (CHIPS, 2)
    scratch = (
        [pltpu.SMEM(a.shape, jnp.int32) for a in (lengths, tile_request, tile_position)]
        + [pltpu.VMEM((2, HEADS * HEAD), bf16)] * 2
        + [pltpu.VMEM((2, HEADS, HEAD), f32)] * 2
        + [pltpu.SMEM((REQUESTS,), jnp.int32)]
        + each(bf16, lambda w, r, n: (2, r, HEAD))
        + each(bf16, lambda w, r, n: (2, *sums, r, HEAD))
        + each(bf16, lambda w, r, n: (SLOTS, TILE, w * HEAD)) * 2
        + each(f32, lambda w, r, n: (SLOTS, r, TILE))
        + each(f32, lambda w, r, n: (SLOTS, r, HEAD))
        + each(f32, lambda w, r, n: (r, 128)) * 2
        + each(bf16, lambda w, r, n: (*sums, r, HEAD)) * 2
        + each(bf16, lambda w, r, n: (CHIPS, n, HEAD)) * 2
        + each(bf16, lambda w, r, n: (2, r, HEAD))
        + [dma, dma, dma((3,)), dma((PHASES, 2))] + [dma((PHASES,))] * 10 + [dma]
    )
    attended, handed = pl.pallas_call(
        kernel,
        out_shape=(pltpu.VMEM((2, HEADS, HEAD), bf16),) * 2,
        in_specs=[any_spec] * 7,
        out_specs=[vmem_spec] * 2,
        scratch_shapes=scratch,
        compiler_params=pltpu.CompilerParams(
            collective_id=0, has_side_effects=True, vmem_limit_bytes=60 * 1024 * 1024),
    )(queries, residual, key_tile_store, value_tile_store, lengths, tile_request, tile_position)
    return attended.reshape(queries.shape), handed.reshape(queries.shape)


def solution(mesh):
    in_specs = (
        P(("section", "peer"), None),
        P(("section", "peer"), None),
        P("section", "peer", None, None),
        P("section", "peer", None, None),
        P("section", None),
        P("section", "peer"),
        P("section", "peer"),
    )
    out_specs = (P(("section", "peer"), None), P(("section", "peer"), None))
    return jax.shard_map(local, mesh=mesh, in_specs=in_specs, out_specs=out_specs, check_vma=False)
```

```python
import jax
import jax.numpy as jnp
from jax import lax
from jax.experimental import pallas as pl
from jax.experimental.pallas import tpu as pltpu
from jax.sharding import PartitionSpec as P

PEERS = 16
CHIPS = 8
SECTIONS = 8
SLOTS = 16
TILE = 256
HEADS = 128
HEAD = 128
REQUESTS = 32
GROUP = 16
WIDTHS = (2, 2, 2, 2)
PHASES = len(WIDTHS)
LAST = PHASES - 1
FIRST = [sum(WIDTHS[:p]) for p in range(PHASES)]
ROWS = [GROUP * w for w in WIDTHS]
SCALE = HEAD ** (-0.5)
NONE = -1e30
STEPS = ((1, 2), (1, 1), (1, 3), (1, 0), (0, 2), (0, 1), (0, 3))
MESH = pl.DeviceIdType.MESH


def landed(ref, sem):
    pltpu.make_async_copy(ref, ref, sem).wait()


def kernel(
    q_hbm, res_hbm, k_hbm, v_hbm, len_hbm, req_hbm, pos_hbm,
    att_ref, nxt_ref,
    len_ref, req_ref, pos_ref, q_in, res_in, q_f32, res_f32, res_send, prev_res, y_got, ym_got, place, *rest,
):
    q_send, gq, kbuf, vbuf, scores, sums_of, meta_own, twin_meta, twin_send, twin_x, x_send, xr, m_send, mr, hand_send = (
        rest[i * PHASES:(i + 1) * PHASES] for i in range(15))
    (
        q_sem, res_sem, plan_sem, kv_sem, gq_send_sem, gq_recv_sem, gq_twin_sem,
        twin_x_send_sem, twin_x_sem, twin_m_send_sem, twin_m_sem,
        x_send_sem, x_sem, m_send_sem, m_sem, hand_send_sem, hand_sem,
        res_send_sem, prev_res_sem, y_send_sem, y_sem, ym_send_sem, ym_sem,
    ) = rest[15 * PHASES:]
    me = lax.axis_index("peer")
    section = lax.axis_index("section")
    core, chip = lax.rem(me, 2), me // 2
    y, z = chip // 4, lax.rem(chip, 4)
    others = [lax.rem(y + dy, 2) * 4 + lax.rem(z + dz, 4) for dy, dz in STEPS]
    twin = me + 1 - 2 * core
    after = lax.rem(section + 1, SECTIONS)
    before = lax.rem(section + SECTIONS - 1, SECTIONS)

    barrier = pltpu.get_barrier_semaphore()

    for to in others:
        pl.semaphore_signal(
            barrier, inc=1, device_id=(section, 2 * to + core), device_id_type=MESH)
    pl.semaphore_signal(barrier, inc=1, device_id=(before, me), device_id_type=MESH)
    pl.semaphore_signal(barrier, inc=1, device_id=(section, twin), device_id_type=MESH)

    q_copy = pltpu.make_async_copy(q_hbm, q_in, q_sem)
    q_copy.start()
    res_copy = pltpu.make_async_copy(res_hbm, res_in, res_sem)
    res_copy.start()
    plan = []
    for i, (src, dst) in enumerate(((len_hbm, len_ref), (req_hbm, req_ref), (pos_hbm, pos_ref))):
        plan.append(pltpu.make_async_copy(src, dst, plan_sem.at[i]))
        plan[i].start()
    def spread(rows, out):
        for h in range(HEADS):
            piece = rows[:, h * HEAD:(h + 1) * HEAD].astype(jnp.float32)
            out[0, h:h + 1, :] = piece[0:1]
            out[1, h:h + 1, :] = piece[1:2]

    q_copy.wait()
    spread(q_in, q_f32)
    for p in range(PHASES):
        q_send[p][...] = q_f32[:, GROUP * FIRST[p]:GROUP * FIRST[p] + ROWS[p], :].astype(jnp.bfloat16)

    pl.semaphore_wait(barrier, CHIPS + 1)

    for p in range(PHASES):
        for to in others:
            pltpu.make_async_remote_copy(
                src_ref=q_send[p], dst_ref=gq[p].at[core, chip],
                send_sem=gq_send_sem.at[p], recv_sem=gq_recv_sem.at[p],
                device_id=(section, 2 * to + core), device_id_type=MESH).start()
        pltpu.make_async_copy(q_send[p], gq[p].at[core, chip], gq_recv_sem.at[p]).start()
    loads = []
    for p in range(PHASES):
        cols = pl.ds(FIRST[p] * HEAD, WIDTHS[p] * HEAD)
        for i, (src, dst) in enumerate(((k_hbm, kbuf), (v_hbm, vbuf))):
            load = pltpu.make_async_copy(
                src.at[0, :, :, cols], dst[p], kv_sem.at[p, i])
            load.start()
            loads.append(load)

    def pass_queries(p):
        landed(gq[p].at[core], gq_recv_sem.at[p])
        copy = pltpu.make_async_remote_copy(
            src_ref=gq[p].at[core], dst_ref=gq[p].at[core],
            send_sem=gq_send_sem.at[p], recv_sem=gq_twin_sem.at[p],
            device_id=(section, twin), device_id_type=MESH)
        copy.start()
        return copy

    res_copy.wait()
    spread(res_in, res_f32)
    res_send[...] = res_f32[:, GROUP * FIRST[LAST]:, :].astype(jnp.bfloat16)
    pass_residual = pltpu.make_async_remote_copy(
        src_ref=res_send, dst_ref=prev_res, send_sem=res_send_sem, recv_sem=prev_res_sem,
        device_id=(after, me), device_id_type=MESH)
    pass_residual.start()
    for copy in plan:
        copy.wait()

    token = lax.broadcasted_iota(jnp.int32, (1, TILE), 1)
    owner = [req_ref[0, t] for t in range(SLOTS)]
    limit = [len_ref[0, owner[t]] - pos_ref[0, t] * TILE for t in range(SLOTS)]
    same = [owner[t] == owner[t - 1] for t in range(1, SLOTS)]
    last = [jnp.where(same[t], -1, owner[t]) for t in range(SLOTS - 1)] + [owner[SLOTS - 1]]
    for r in range(REQUESTS):
        at = jnp.int32(0)
        for t in range(SLOTS):
            at = jnp.where(last[t] == r, t, at)
        place[r] = at
    column = [
        jnp.where(r < 0, -128, ((r >> 1) & 1) * 64 + (r & 1) * 8 + (r >> 2)) for r in last]

    def lanes(p):
        return lax.broadcasted_iota(jnp.int32, (ROWS[p], 128), 1)

    def attend(p):
        lane = lanes(p)
        tops = []
        for t in range(SLOTS):
            r = owner[t]
            q = gq[p][(r >> 1) & 1, r >> 2, r & 1]
            score = jnp.concatenate(
                [lax.dot_general(
                    q[GROUP * g:GROUP * (g + 1)], kbuf[p][t, :, HEAD * g:HEAD * (g + 1)],
                    (((1,), (1,)), ((), ())), preferred_element_type=jnp.float32)
                 for g in range(WIDTHS[p])], axis=0) * SCALE
            score = jnp.where(token < limit[t], score, -jnp.inf)
            scores[p][t] = score
            tops.append(jnp.max(
                jnp.maximum(score[:, :128], score[:, 128:]), axis=1, keepdims=True))
        for t in range(1, SLOTS):
            tops[t] = jnp.maximum(jnp.where(same[t - 1], tops[t - 1], -jnp.inf), tops[t])
        for t in range(SLOTS - 2, -1, -1):
            tops[t] = jnp.where(same[t], tops[t + 1], tops[t])
        mix, total = None, None
        meta = jnp.where((lane & 63) < 16, NONE, 0.0)
        for t in range(SLOTS):
            weight = jnp.exp(scores[p][t] - tops[t]).astype(jnp.bfloat16)
            part = jnp.concatenate(
                [jnp.dot(
                    weight[GROUP * g:GROUP * (g + 1)], vbuf[p][t, :, HEAD * g:HEAD * (g + 1)],
                    preferred_element_type=jnp.float32)
                 for g in range(WIDTHS[p])], axis=0)
            wide = weight.astype(jnp.float32)
            count = jnp.sum(wide[:, :128] + wide[:, 128:], axis=1, keepdims=True)
            mix = part if t == 0 else jnp.where(same[t - 1], mix, 0.0) + part
            total = count if t == 0 else jnp.where(same[t - 1], total, 0.0) + count
            sums_of[p][t] = mix
            meta = jnp.where(lane == column[t], tops[t], meta)
            meta = jnp.where(lane == column[t] + 16, total, meta)
        meta_own[p][...] = meta
        pltpu.make_async_remote_copy(
            src_ref=meta_own[p], dst_ref=twin_meta[p],
            send_sem=twin_m_send_sem.at[p], recv_sem=twin_m_sem.at[p],
            device_id=(section, twin), device_id_type=MESH).start()
        for c in range(CHIPS):
            for i in range(2):
                twin_send[p][c, i] = sums_of[p][place[4 * c + 2 * (1 - core) + i]].astype(jnp.bfloat16)
        pltpu.make_async_remote_copy(
            src_ref=twin_send[p], dst_ref=twin_x[p],
            send_sem=twin_x_send_sem.at[p], recv_sem=twin_x_sem.at[p],
            device_id=(section, twin), device_id_type=MESH).start()

    def join_cores(p):
        lane, rows = lanes(p), ROWS[p]
        landed(twin_meta[p], twin_m_sem.at[p])
        here = pltpu.roll(meta_own[p][...], 64 * core, 1)
        there = pltpu.roll(twin_meta[p][...], 64 * core, 1)
        peak = jnp.maximum(here, there)
        by_here, by_there = jnp.exp(here - peak), jnp.exp(there - peak)
        total = by_here * pltpu.roll(here, 112, 1) + by_there * pltpu.roll(there, 112, 1)
        meta = jnp.where(lane < 16, peak, jnp.where(lane < 32, pltpu.roll(total, 16, 1), 0.0))
        turned = jnp.concatenate([meta, jnp.zeros((128 - rows, 128), jnp.float32)], axis=0).T
        table = jnp.concatenate([turned[CHIPS * i:CHIPS * (i + 1), :rows] for i in range(4)], axis=1)
        for c in range(CHIPS):
            m_send[p][c] = table[c:c + 1]
        landed(twin_x[p], twin_x_sem.at[p])
        for c in range(CHIPS):
            for i in range(2):
                at = 8 * i + c
                own = sums_of[p][place[4 * c + 2 * core + i]]
                other = twin_x[p][c, i].astype(jnp.float32)
                x_send[p][c, i] = (
                    by_here[:, at:at + 1] * own + by_there[:, at:at + 1] * other).astype(jnp.bfloat16)
        if p == LAST:
            for to in others + [chip]:
                pltpu.make_async_remote_copy(
                    src_ref=x_send[p].at[to], dst_ref=y_got.at[chip],
                    send_sem=y_send_sem, recv_sem=y_sem,
                    device_id=(after, 2 * to + core), device_id_type=MESH).start()
                pltpu.make_async_remote_copy(
                    src_ref=m_send[p].at[to], dst_ref=ym_got.at[chip],
                    send_sem=ym_send_sem, recv_sem=ym_sem,
                    device_id=(after, 2 * to + core), device_id_type=MESH).start()
        for to in others:
            pltpu.make_async_remote_copy(
                src_ref=x_send[p].at[to], dst_ref=xr[p].at[chip],
                send_sem=x_send_sem.at[p], recv_sem=x_sem.at[p],
                device_id=(section, 2 * to + core), device_id_type=MESH).start()
            pltpu.make_async_remote_copy(
                src_ref=m_send[p].at[to], dst_ref=mr[p].at[chip],
                send_sem=m_send_sem.at[p], recv_sem=m_sem.at[p],
                device_id=(section, 2 * to + core), device_id_type=MESH).start()
        pltpu.make_async_copy(x_send[p].at[chip], xr[p].at[chip], x_sem.at[p]).start()
        pltpu.make_async_copy(m_send[p].at[chip], mr[p].at[chip], m_sem.at[p]).start()

    def join_chips(p, got, got_sem, lines, lines_sem, finish):
        lane, rows = lanes(p), ROWS[p]
        landed(lines, lines_sem)
        table = jnp.concatenate([lines[c] for c in range(CHIPS)], axis=0)
        kinds = jnp.concatenate([table[:, rows * i:rows * (i + 1)] for i in range(4)], axis=0)
        kinds = jnp.concatenate([kinds, jnp.zeros((32, 128 - rows), jnp.float32)], axis=1)
        meta = jnp.concatenate([kinds, jnp.zeros((128 - 32, 128), jnp.float32)], axis=0).T[:rows]
        totals = pltpu.roll(meta, 112, 1)
        landed(got, got_sem)
        for i in range(2):
            used = (lane >> 3) == i
            peaks = jnp.where(used, meta, NONE)
            part = jnp.exp(peaks - jnp.max(peaks, axis=1, keepdims=True))
            whole = jnp.sum(jnp.where(used, part * totals, 0.0), axis=1, keepdims=True)
            part = part / whole
            mix = None
            for c in range(CHIPS):
                at = 8 * i + c
                term = part[:, at:at + 1] * got[c, i].astype(jnp.float32)
                mix = term if mix is None else mix + term
            finish(i, mix.astype(jnp.bfloat16))

    def finish_here(p):
        heads = pl.ds(GROUP * FIRST[p], ROWS[p])

        def finish(i, attended):
            att_ref[i, heads, :] = attended
            if p < LAST:
                hand_send[p][i] = (
                    res_f32[i, heads, :] + attended.astype(jnp.float32)).astype(jnp.bfloat16)

        join_chips(p, xr[p], x_sem.at[p], mr[p], m_sem.at[p], finish)
        if p < LAST:
            pltpu.make_async_remote_copy(
                src_ref=hand_send[p], dst_ref=nxt_ref.at[:, heads, :],
                send_sem=hand_send_sem.at[p], recv_sem=hand_sem,
                device_id=(after, me), device_id_type=MESH).start()

    def finish_before():
        def finish(i, attended):
            nxt_ref[i, GROUP * FIRST[LAST]:, :] = (
                prev_res[i].astype(jnp.float32) + attended.astype(jnp.float32)).astype(jnp.bfloat16)

        join_chips(LAST, y_got, y_sem, ym_got, ym_sem, finish)

    passed = [pass_queries(0), pass_queries(1)]
    for p in range(PHASES):
        passed[p].wait_recv()
        loads[2 * p].wait()
        loads[2 * p + 1].wait()
        attend(p)
        if p + 2 < PHASES:
            passed.append(pass_queries(p + 2))
        if p > 0:
            join_cores(p - 1)
    join_cores(PHASES - 1)
    for p in range(PHASES):
        finish_here(p)
    pass_residual.wait()
    finish_before()

    for p in range(PHASES):
        landed(gq[p].at[0, pl.ds(0, 7)], gq_send_sem.at[p])
        landed(gq[p].at[0], gq_send_sem.at[p])
        landed(x_send[p].at[pl.ds(0, 7)], x_send_sem.at[p])
        landed(m_send[p].at[pl.ds(0, 7)], m_send_sem.at[p])
        landed(twin_send[p], twin_x_send_sem.at[p])
        landed(meta_own[p], twin_m_send_sem.at[p])
        if p < LAST:
            landed(hand_send[p], hand_send_sem.at[p])
    landed(x_send[LAST], y_send_sem)
    landed(m_send[LAST], ym_send_sem)
    landed(nxt_ref.at[:, pl.ds(0, GROUP * FIRST[LAST]), :], hand_sem)


def local(
    queries, residual, key_tile_store, value_tile_store, lengths, tile_request, tile_position
):
    any_spec = pl.BlockSpec(memory_space=pl.ANY)
    vmem_spec = pl.BlockSpec(memory_space=pltpu.VMEM)
    dma = pltpu.SemaphoreType.DMA
    bf16, f32 = jnp.bfloat16, jnp.float32
    def each(dtype, shape):
        return [pltpu.VMEM(shape(w, r), dtype) for w, r in zip(WIDTHS, ROWS, strict=True)]

    sums = (CHIPS, 2)
    scratch = (
        [pltpu.SMEM(a.shape, jnp.int32) for a in (lengths, tile_request, tile_position)]
        + [pltpu.VMEM((2, HEADS * HEAD), bf16)] * 2
        + [pltpu.VMEM((2, HEADS, HEAD), f32)] * 2
        + [pltpu.VMEM((2, ROWS[LAST], HEAD), bf16)] * 2
        + [pltpu.VMEM((CHIPS, 2, ROWS[LAST], HEAD), bf16), pltpu.VMEM((CHIPS, 1, 4 * ROWS[LAST]), f32)]
        + [pltpu.SMEM((REQUESTS,), jnp.int32)]
        + each(bf16, lambda w, r: (2, r, HEAD))
        + each(bf16, lambda w, r: (2, *sums, r, HEAD))
        + each(bf16, lambda w, r: (SLOTS, TILE, w * HEAD)) * 2
        + each(f32, lambda w, r: (SLOTS, r, TILE))
        + each(f32, lambda w, r: (SLOTS, r, HEAD))
        + each(f32, lambda w, r: (r, 128)) * 2
        + each(bf16, lambda w, r: (*sums, r, HEAD)) * 2
        + each(bf16, lambda w, r: (*sums, r, HEAD)) * 2
        + each(f32, lambda w, r: (CHIPS, 1, 4 * r)) * 2
        + each(bf16, lambda w, r: (2, r, HEAD))
        + [dma, dma, dma((3,)), dma((PHASES, 2))] + [dma((PHASES,))] * 12 + [dma] * 7
    )
    attended, handed = pl.pallas_call(
        kernel,
        out_shape=(pltpu.VMEM((2, HEADS, HEAD), bf16),) * 2,
        in_specs=[any_spec] * 7,
        out_specs=[vmem_spec] * 2,
        scratch_shapes=scratch,
        compiler_params=pltpu.CompilerParams(
            collective_id=0, has_side_effects=True, vmem_limit_bytes=60 * 1024 * 1024),
    )(queries, residual, key_tile_store, value_tile_store, lengths, tile_request, tile_position)
    return attended.reshape(queries.shape), handed.reshape(queries.shape)


def solution(mesh):
    in_specs = (
        P(("section", "peer"), None),
        P(("section", "peer"), None),
        P("section", "peer", None, None),
        P("section", "peer", None, None),
        P("section", None),
        P("section", "peer"),
        P("section", "peer"),
    )
    out_specs = (P(("section", "peer"), None), P(("section", "peer"), None))
    return jax.shard_map(local, mesh=mesh, in_specs=in_specs, out_specs=out_specs, check_vma=False)
```

```python
import jax
import jax.numpy as jnp
from jax import lax
from jax.experimental import pallas as pl
from jax.experimental.pallas import tpu as pltpu
from jax.sharding import PartitionSpec as P

PEERS = 16
CHIPS = 8
SECTIONS = 8
SLOTS = 16
TILE = 256
HEADS = 128
HEAD = 128
REQUESTS = 32
GROUP = 16
WIDTHS = (2, 2, 2, 2)
PHASES = len(WIDTHS)
TWICE = 3
EARLY = 1
LAST = PHASES - 1
FIRST = [sum(WIDTHS[:p]) for p in range(PHASES)]
ROWS = [GROUP * w for w in WIDTHS]
SCALE = HEAD ** (-0.5)
NONE = -1e30
STEPS = ((1, 2), (1, 1), (1, 3), (1, 0), (0, 2), (0, 1), (0, 3))
MESH = pl.DeviceIdType.MESH


def widen(block):
    rest = 128 - block.shape[1]
    if not rest:
        return block
    return jnp.concatenate([block, jnp.zeros((block.shape[0], rest), block.dtype)], axis=1)


def landed(ref, sem):
    pltpu.make_async_copy(ref, ref, sem).wait()


def kernel(
    q_hbm, res_hbm, k_hbm, v_hbm, len_hbm, req_hbm, pos_hbm,
    att_ref, nxt_ref,
    len_ref, req_ref, pos_ref, q_in, res_in, q_f32, res_f32, res_send, prev_res, place, *rest,
):
    q_send, gq, kbuf, vbuf, scores, sums_of, meta_own, twin_meta, twin_send, twin_x, x_send, xr, m_send, mr, hand_send = (
        rest[i * PHASES:(i + 1) * PHASES] for i in range(15))
    (
        q_sem, res_sem, plan_sem, kv_sem, gq_send_sem, gq_recv_sem, gq_twin_sem,
        twin_x_send_sem, twin_x_sem, twin_m_send_sem, twin_m_sem,
        x_send_sem, x_sem, m_send_sem, m_sem, hand_send_sem, hand_sem,
        res_send_sem, prev_res_sem, y_send_sem, y_sem, ym_send_sem, ym_sem,
    ) = rest[15 * PHASES + 2 * (PHASES - TWICE):]
    y_got = rest[15 * PHASES:][:PHASES - TWICE]
    ym_got = rest[15 * PHASES:][PHASES - TWICE:2 * (PHASES - TWICE)]
    me = lax.axis_index("peer")
    section = lax.axis_index("section")
    core, chip = lax.rem(me, 2), me // 2
    y, z = chip // 4, lax.rem(chip, 4)
    others = [lax.rem(y + dy, 2) * 4 + lax.rem(z + dz, 4) for dy, dz in STEPS]
    twin = me + 1 - 2 * core
    after = lax.rem(section + 1, SECTIONS)
    before = lax.rem(section + SECTIONS - 1, SECTIONS)

    barrier = pltpu.get_barrier_semaphore()

    for to in others:
        pl.semaphore_signal(
            barrier, inc=1, device_id=(section, 2 * to + core), device_id_type=MESH)
    pl.semaphore_signal(barrier, inc=1, device_id=(before, me), device_id_type=MESH)
    pl.semaphore_signal(barrier, inc=1, device_id=(section, twin), device_id_type=MESH)

    q_copy = pltpu.make_async_copy(q_hbm, q_in, q_sem)
    q_copy.start()
    res_copy = pltpu.make_async_copy(res_hbm, res_in, res_sem)
    res_copy.start()
    plan = []
    for i, (src, dst) in enumerate(((len_hbm, len_ref), (req_hbm, req_ref), (pos_hbm, pos_ref))):
        plan.append(pltpu.make_async_copy(src, dst, plan_sem.at[i]))
        plan[i].start()
    def spread(rows, out):
        for h in range(HEADS):
            piece = rows[:, h * HEAD:(h + 1) * HEAD].astype(jnp.float32)
            out[0, h:h + 1, :] = piece[0:1]
            out[1, h:h + 1, :] = piece[1:2]

    q_copy.wait()
    spread(q_in, q_f32)
    for p in range(PHASES):
        q_send[p][...] = q_f32[:, GROUP * FIRST[p]:GROUP * FIRST[p] + ROWS[p], :].astype(jnp.bfloat16)

    pl.semaphore_wait(barrier, CHIPS + 1)

    for p in range(PHASES):
        for to in others:
            pltpu.make_async_remote_copy(
                src_ref=q_send[p], dst_ref=gq[p].at[core, chip],
                send_sem=gq_send_sem.at[p], recv_sem=gq_recv_sem.at[p],
                device_id=(section, 2 * to + core), device_id_type=MESH).start()
        pltpu.make_async_copy(q_send[p], gq[p].at[core, chip], gq_recv_sem.at[p]).start()
    loads = []
    for p in range(PHASES):
        cols = pl.ds(FIRST[p] * HEAD, WIDTHS[p] * HEAD)
        for i, (src, dst) in enumerate(((k_hbm, kbuf), (v_hbm, vbuf))):
            load = pltpu.make_async_copy(
                src.at[0, :, :, cols], dst[p], kv_sem.at[p, i])
            load.start()
            loads.append(load)

    def pass_queries(p):
        landed(gq[p].at[core], gq_recv_sem.at[p])
        copy = pltpu.make_async_remote_copy(
            src_ref=gq[p].at[core], dst_ref=gq[p].at[core],
            send_sem=gq_send_sem.at[p], recv_sem=gq_twin_sem.at[p],
            device_id=(section, twin), device_id_type=MESH)
        copy.start()
        return copy

    res_copy.wait()
    spread(res_in, res_f32)
    res_send[...] = res_f32[:, GROUP * FIRST[TWICE]:, :].astype(jnp.bfloat16)
    pass_residual = pltpu.make_async_remote_copy(
        src_ref=res_send, dst_ref=prev_res, send_sem=res_send_sem, recv_sem=prev_res_sem,
        device_id=(after, me), device_id_type=MESH)
    pass_residual.start()
    for copy in plan:
        copy.wait()

    token = lax.broadcasted_iota(jnp.int32, (1, TILE), 1)
    owner = [req_ref[0, t] for t in range(SLOTS)]
    limit = [len_ref[0, owner[t]] - pos_ref[0, t] * TILE for t in range(SLOTS)]
    same = [owner[t] == owner[t - 1] for t in range(1, SLOTS)]
    last = [jnp.where(same[t], -1, owner[t]) for t in range(SLOTS - 1)] + [owner[SLOTS - 1]]
    for r in range(REQUESTS):
        at = jnp.int32(0)
        for t in range(SLOTS):
            at = jnp.where(last[t] == r, t, at)
        place[r] = at
    column = [
        jnp.where(r < 0, -128, ((r >> 1) & 1) * 64 + (r & 1) * 8 + (r >> 2)) for r in last]

    def lanes(p):
        return lax.broadcasted_iota(jnp.int32, (ROWS[p], 128), 1)

    def attend(p):
        lane = lanes(p)
        tops = []
        for t in range(SLOTS):
            r = owner[t]
            q = gq[p][(r >> 1) & 1, r >> 2, r & 1]
            score = jnp.concatenate(
                [lax.dot_general(
                    q[GROUP * g:GROUP * (g + 1)], kbuf[p][t, :, HEAD * g:HEAD * (g + 1)],
                    (((1,), (1,)), ((), ())), preferred_element_type=jnp.float32)
                 for g in range(WIDTHS[p])], axis=0) * SCALE
            score = jnp.where(token < limit[t], score, -jnp.inf)
            scores[p][t] = score
            tops.append(jnp.max(
                jnp.maximum(score[:, :128], score[:, 128:]), axis=1, keepdims=True))
        for t in range(1, SLOTS):
            tops[t] = jnp.maximum(jnp.where(same[t - 1], tops[t - 1], -jnp.inf), tops[t])
        for t in range(SLOTS - 2, -1, -1):
            tops[t] = jnp.where(same[t], tops[t + 1], tops[t])
        mix, total = None, None
        meta = jnp.where((lane & 63) < 16, NONE, 0.0)
        for t in range(SLOTS):
            weight = jnp.exp(scores[p][t] - tops[t]).astype(jnp.bfloat16)
            part = jnp.concatenate(
                [jnp.dot(
                    weight[GROUP * g:GROUP * (g + 1)], vbuf[p][t, :, HEAD * g:HEAD * (g + 1)],
                    preferred_element_type=jnp.float32)
                 for g in range(WIDTHS[p])], axis=0)
            wide = weight.astype(jnp.float32)
            count = jnp.sum(wide[:, :128] + wide[:, 128:], axis=1, keepdims=True)
            mix = part if t == 0 else jnp.where(same[t - 1], mix, 0.0) + part
            total = count if t == 0 else jnp.where(same[t - 1], total, 0.0) + count
            sums_of[p][t] = mix
            meta = jnp.where(lane == column[t], tops[t], meta)
            meta = jnp.where(lane == column[t] + 16, total, meta)
        meta_own[p][...] = meta
        pltpu.make_async_remote_copy(
            src_ref=meta_own[p], dst_ref=twin_meta[p],
            send_sem=twin_m_send_sem.at[p], recv_sem=twin_m_sem.at[p],
            device_id=(section, twin), device_id_type=MESH).start()
        for c in range(CHIPS):
            for i in range(2):
                twin_send[p][c, i] = sums_of[p][place[4 * c + 2 * (1 - core) + i]].astype(jnp.bfloat16)
        pltpu.make_async_remote_copy(
            src_ref=twin_send[p], dst_ref=twin_x[p],
            send_sem=twin_x_send_sem.at[p], recv_sem=twin_x_sem.at[p],
            device_id=(section, twin), device_id_type=MESH).start()

    def join_cores(p):
        lane, rows = lanes(p), ROWS[p]
        landed(twin_meta[p], twin_m_sem.at[p])
        here = pltpu.roll(meta_own[p][...], 64 * core, 1)
        there = pltpu.roll(twin_meta[p][...], 64 * core, 1)
        peak = jnp.maximum(here, there)
        by_here, by_there = jnp.exp(here - peak), jnp.exp(there - peak)
        total = by_here * pltpu.roll(here, 112, 1) + by_there * pltpu.roll(there, 112, 1)
        meta = jnp.where(lane < 16, peak, jnp.where(lane < 32, pltpu.roll(total, 16, 1), 0.0))
        turned = jnp.concatenate([meta, jnp.zeros((128 - rows, 128), jnp.float32)], axis=0).T
        table = widen(jnp.concatenate(
            [turned[CHIPS * i:CHIPS * (i + 1), :rows] for i in range(4)], axis=1))
        for c in range(CHIPS):
            m_send[p][c] = table[c:c + 1]
        landed(twin_x[p], twin_x_sem.at[p])
        for c in range(CHIPS):
            for i in range(2):
                at = 8 * i + c
                own = sums_of[p][place[4 * c + 2 * core + i]]
                other = twin_x[p][c, i].astype(jnp.float32)
                x_send[p][c, i] = (
                    by_here[:, at:at + 1] * own + by_there[:, at:at + 1] * other).astype(jnp.bfloat16)
        if p >= TWICE:
            for to in others + [chip]:
                pltpu.make_async_remote_copy(
                    src_ref=x_send[p].at[to], dst_ref=y_got[p - TWICE].at[chip],
                    send_sem=y_send_sem.at[p - TWICE], recv_sem=y_sem.at[p - TWICE],
                    device_id=(after, 2 * to + core), device_id_type=MESH).start()
                pltpu.make_async_remote_copy(
                    src_ref=m_send[p].at[to], dst_ref=ym_got[p - TWICE].at[chip],
                    send_sem=ym_send_sem.at[p - TWICE], recv_sem=ym_sem.at[p - TWICE],
                    device_id=(after, 2 * to + core), device_id_type=MESH).start()
        for to in others:
            pltpu.make_async_remote_copy(
                src_ref=x_send[p].at[to], dst_ref=xr[p].at[chip],
                send_sem=x_send_sem.at[p], recv_sem=x_sem.at[p],
                device_id=(section, 2 * to + core), device_id_type=MESH).start()
            pltpu.make_async_remote_copy(
                src_ref=m_send[p].at[to], dst_ref=mr[p].at[chip],
                send_sem=m_send_sem.at[p], recv_sem=m_sem.at[p],
                device_id=(section, 2 * to + core), device_id_type=MESH).start()
        pltpu.make_async_copy(x_send[p].at[chip], xr[p].at[chip], x_sem.at[p]).start()
        pltpu.make_async_copy(m_send[p].at[chip], mr[p].at[chip], m_sem.at[p]).start()

    def join_chips(p, got, got_sem, lines, lines_sem, finish):
        lane, rows = lanes(p), ROWS[p]
        landed(lines, lines_sem)
        table = jnp.concatenate([lines[c] for c in range(CHIPS)], axis=0)
        kinds = jnp.concatenate([table[:, rows * i:rows * (i + 1)] for i in range(4)], axis=0)
        kinds = jnp.concatenate([kinds, jnp.zeros((32, 128 - rows), jnp.float32)], axis=1)
        meta = jnp.concatenate([kinds, jnp.zeros((128 - 32, 128), jnp.float32)], axis=0).T[:rows]
        totals = pltpu.roll(meta, 112, 1)
        landed(got, got_sem)
        for i in range(2):
            used = (lane >> 3) == i
            peaks = jnp.where(used, meta, NONE)
            part = jnp.exp(peaks - jnp.max(peaks, axis=1, keepdims=True))
            whole = jnp.sum(jnp.where(used, part * totals, 0.0), axis=1, keepdims=True)
            part = part / whole
            mix = None
            for c in range(CHIPS):
                at = 8 * i + c
                term = part[:, at:at + 1] * got[c, i].astype(jnp.float32)
                mix = term if mix is None else mix + term
            finish(i, mix.astype(jnp.bfloat16))

    def finish_here(p):
        heads = pl.ds(GROUP * FIRST[p], ROWS[p])

        def finish(i, attended):
            att_ref[i, heads, :] = attended
            if p < TWICE:
                hand_send[p][i] = (
                    res_f32[i, heads, :] + attended.astype(jnp.float32)).astype(jnp.bfloat16)

        join_chips(p, xr[p], x_sem.at[p], mr[p], m_sem.at[p], finish)
        if p < TWICE:
            pltpu.make_async_remote_copy(
                src_ref=hand_send[p], dst_ref=nxt_ref.at[:, heads, :],
                send_sem=hand_send_sem.at[p], recv_sem=hand_sem,
                device_id=(after, me), device_id_type=MESH).start()

    def finish_before(p):
        heads = pl.ds(GROUP * FIRST[p], ROWS[p])
        rows = pl.ds(GROUP * (FIRST[p] - FIRST[TWICE]), ROWS[p])
        k = p - TWICE

        def finish(i, attended):
            nxt_ref[i, heads, :] = (
                prev_res[i, rows, :].astype(jnp.float32) + attended.astype(jnp.float32)).astype(jnp.bfloat16)

        join_chips(p, y_got[k], y_sem.at[k], ym_got[k], ym_sem.at[k], finish)

    passed = [pass_queries(0), pass_queries(1)]
    for p in range(PHASES):
        passed[p].wait_recv()
        loads[2 * p].wait()
        loads[2 * p + 1].wait()
        attend(p)
        if p + 2 < PHASES:
            passed.append(pass_queries(p + 2))
        if p > 0:
            join_cores(p - 1)
    for p in range(EARLY):
        finish_here(p)
    join_cores(LAST)
    for p in range(EARLY, PHASES):
        finish_here(p)
        if p == TWICE - 1:
            pass_residual.wait()
        if p >= TWICE:
            finish_before(p)

    for p in range(PHASES):
        landed(gq[p].at[0, pl.ds(0, 7)], gq_send_sem.at[p])
        landed(gq[p].at[0], gq_send_sem.at[p])
        landed(x_send[p].at[pl.ds(0, 7)], x_send_sem.at[p])
        landed(m_send[p].at[pl.ds(0, 7)], m_send_sem.at[p])
        landed(twin_send[p], twin_x_send_sem.at[p])
        landed(meta_own[p], twin_m_send_sem.at[p])
        if p < TWICE:
            landed(hand_send[p], hand_send_sem.at[p])
    for p in range(TWICE, PHASES):
        landed(x_send[p], y_send_sem.at[p - TWICE])
        landed(m_send[p], ym_send_sem.at[p - TWICE])
    landed(nxt_ref.at[:, pl.ds(0, GROUP * FIRST[TWICE]), :], hand_sem)


def local(
    queries, residual, key_tile_store, value_tile_store, lengths, tile_request, tile_position
):
    any_spec = pl.BlockSpec(memory_space=pl.ANY)
    vmem_spec = pl.BlockSpec(memory_space=pltpu.VMEM)
    dma = pltpu.SemaphoreType.DMA
    bf16, f32 = jnp.bfloat16, jnp.float32
    def each(dtype, shape):
        return [pltpu.VMEM(shape(w, r), dtype) for w, r in zip(WIDTHS, ROWS, strict=True)]

    sums = (CHIPS, 2)
    scratch = (
        [pltpu.SMEM(a.shape, jnp.int32) for a in (lengths, tile_request, tile_position)]
        + [pltpu.VMEM((2, HEADS * HEAD), bf16)] * 2
        + [pltpu.VMEM((2, HEADS, HEAD), f32)] * 2
        + [pltpu.VMEM((2, HEADS - GROUP * FIRST[TWICE], HEAD), bf16)] * 2
        + [pltpu.SMEM((REQUESTS,), jnp.int32)]
        + each(bf16, lambda w, r: (2, r, HEAD))
        + each(bf16, lambda w, r: (2, *sums, r, HEAD))
        + each(bf16, lambda w, r: (SLOTS, TILE, w * HEAD)) * 2
        + each(f32, lambda w, r: (SLOTS, r, TILE))
        + each(f32, lambda w, r: (SLOTS, r, HEAD))
        + each(f32, lambda w, r: (r, 128)) * 2
        + each(bf16, lambda w, r: (*sums, r, HEAD)) * 2
        + each(bf16, lambda w, r: (*sums, r, HEAD)) * 2
        + each(f32, lambda w, r: (CHIPS, 1, 128)) * 2
        + each(bf16, lambda w, r: (2, r, HEAD))
        + each(bf16, lambda w, r: (*sums, r, HEAD))[TWICE:]
        + each(f32, lambda w, r: (CHIPS, 1, 128))[TWICE:]
        + [dma, dma, dma((3,)), dma((PHASES, 2))] + [dma((PHASES,))] * 12 + [dma] * 3 + [dma((PHASES - TWICE,))] * 4
    )
    attended, handed = pl.pallas_call(
        kernel,
        out_shape=(pltpu.VMEM((2, HEADS, HEAD), bf16),) * 2,
        in_specs=[any_spec] * 7,
        out_specs=[vmem_spec] * 2,
        scratch_shapes=scratch,
        compiler_params=pltpu.CompilerParams(
            collective_id=0, has_side_effects=True, vmem_limit_bytes=60 * 1024 * 1024),
    )(queries, residual, key_tile_store, value_tile_store, lengths, tile_request, tile_position)
    return attended.reshape(queries.shape), handed.reshape(queries.shape)


def solution(mesh):
    in_specs = (
        P(("section", "peer"), None),
        P(("section", "peer"), None),
        P("section", "peer", None, None),
        P("section", "peer", None, None),
        P("section", None),
        P("section", "peer"),
        P("section", "peer"),
    )
    out_specs = (P(("section", "peer"), None), P(("section", "peer"), None))
    return jax.shard_map(local, mesh=mesh, in_specs=in_specs, out_specs=out_specs, check_vma=False)
```

```python
import jax
import jax.numpy as jnp
from jax import lax
from jax.experimental import pallas as pl
from jax.experimental.pallas import tpu as pltpu
from jax.sharding import PartitionSpec as P

PEERS = 16
CHIPS = 8
SECTIONS = 8
SLOTS = 16
TILE = 256
HEADS = 128
HEAD = 128
REQUESTS = 32
GROUP = 16
WIDTHS = (2, 2, 2, 2)
PHASES = len(WIDTHS)
TWICE = 3
EARLY = 1
LAST = PHASES - 1
FIRST = [sum(WIDTHS[:p]) for p in range(PHASES)]
ROWS = [GROUP * w for w in WIDTHS]
SCALE = HEAD ** (-0.5)
NONE = -1e30
STEPS = ((1, 2), (1, 1), (1, 3), (1, 0), (0, 2), (0, 1), (0, 3))
MESH = pl.DeviceIdType.MESH


def widen(block):
    rest = 128 - block.shape[1]
    if not rest:
        return block
    return jnp.concatenate([block, jnp.zeros((block.shape[0], rest), block.dtype)], axis=1)


def landed(ref, sem):
    pltpu.make_async_copy(ref, ref, sem).wait()


def kernel(
    q_hbm, res_hbm, k_hbm, v_hbm, len_hbm, req_hbm, pos_hbm,
    att_ref, nxt_ref,
    len_ref, req_ref, pos_ref, q_in, res_in, q_f32, res_f32, res_send, prev_res, place, *rest,
):
    q_send, gq, kbuf, vbuf, scores, sums_of, meta_own, twin_meta, twin_send, twin_x, x_send, xr, m_send, mr, hand_send = (
        rest[i * PHASES:(i + 1) * PHASES] for i in range(15))
    (
        q_sem, res_sem, plan_sem, kv_sem, gq_send_sem, gq_recv_sem, gq_twin_sem,
        twin_x_send_sem, twin_x_sem, twin_m_send_sem, twin_m_sem,
        x_send_sem, x_sem, m_send_sem, m_sem, hand_send_sem, hand_sem,
        res_send_sem, prev_res_sem, y_send_sem, y_sem, ym_send_sem, ym_sem,
    ) = rest[15 * PHASES + 2 * (PHASES - TWICE):]
    y_got = rest[15 * PHASES:][:PHASES - TWICE]
    ym_got = rest[15 * PHASES:][PHASES - TWICE:2 * (PHASES - TWICE)]
    me = lax.axis_index("peer")
    section = lax.axis_index("section")
    core, chip = lax.rem(me, 2), me // 2
    y, z = chip // 4, lax.rem(chip, 4)
    others = [lax.rem(y + dy, 2) * 4 + lax.rem(z + dz, 4) for dy, dz in STEPS]
    twin = me + 1 - 2 * core
    after = lax.rem(section + 1, SECTIONS)
    before = lax.rem(section + SECTIONS - 1, SECTIONS)

    barrier = pltpu.get_barrier_semaphore()

    for to in others:
        pl.semaphore_signal(
            barrier, inc=1, device_id=(section, 2 * to + core), device_id_type=MESH)
    pl.semaphore_signal(barrier, inc=1, device_id=(before, me), device_id_type=MESH)
    pl.semaphore_signal(barrier, inc=1, device_id=(section, twin), device_id_type=MESH)

    q_copy = pltpu.make_async_copy(q_hbm, q_in, q_sem)
    q_copy.start()
    res_copy = pltpu.make_async_copy(res_hbm, res_in, res_sem)
    res_copy.start()
    plan = []
    for i, (src, dst) in enumerate(((len_hbm, len_ref), (req_hbm, req_ref), (pos_hbm, pos_ref))):
        plan.append(pltpu.make_async_copy(src, dst, plan_sem.at[i]))
        plan[i].start()
    def spread(rows, out):
        for h in range(HEADS):
            piece = rows[:, h * HEAD:(h + 1) * HEAD].astype(jnp.float32)
            out[0, h:h + 1, :] = piece[0:1]
            out[1, h:h + 1, :] = piece[1:2]

    q_copy.wait()
    spread(q_in, q_f32)
    for p in range(PHASES):
        q_send[p][...] = q_f32[:, GROUP * FIRST[p]:GROUP * FIRST[p] + ROWS[p], :].astype(jnp.bfloat16)

    pl.semaphore_wait(barrier, CHIPS + 1)

    for p in range(PHASES):
        for to in others:
            pltpu.make_async_remote_copy(
                src_ref=q_send[p], dst_ref=gq[p].at[core, chip],
                send_sem=gq_send_sem.at[p], recv_sem=gq_recv_sem.at[p],
                device_id=(section, 2 * to + core), device_id_type=MESH).start()
        pltpu.make_async_copy(q_send[p], gq[p].at[core, chip], gq_recv_sem.at[p]).start()
    loads = []
    for p in range(PHASES):
        cols = pl.ds(FIRST[p] * HEAD, WIDTHS[p] * HEAD)
        for i, (src, dst) in enumerate(((k_hbm, kbuf), (v_hbm, vbuf))):
            load = pltpu.make_async_copy(
                src.at[0, :, :, cols], dst[p], kv_sem.at[p, i])
            load.start()
            loads.append(load)

    def pass_queries(p):
        landed(gq[p].at[core], gq_recv_sem.at[p])
        copy = pltpu.make_async_remote_copy(
            src_ref=gq[p].at[core], dst_ref=gq[p].at[core],
            send_sem=gq_send_sem.at[p], recv_sem=gq_twin_sem.at[p],
            device_id=(section, twin), device_id_type=MESH)
        copy.start()
        return copy

    res_copy.wait()
    spread(res_in, res_f32)
    res_send[...] = res_f32[:, GROUP * FIRST[TWICE]:, :].astype(jnp.bfloat16)
    pass_residual = pltpu.make_async_remote_copy(
        src_ref=res_send, dst_ref=prev_res, send_sem=res_send_sem, recv_sem=prev_res_sem,
        device_id=(after, me), device_id_type=MESH)
    pass_residual.start()
    for copy in plan:
        copy.wait()

    token = lax.broadcasted_iota(jnp.int32, (1, TILE), 1)
    owner = [req_ref[0, t] for t in range(SLOTS)]
    limit = [len_ref[0, owner[t]] - pos_ref[0, t] * TILE for t in range(SLOTS)]
    same = [owner[t] == owner[t - 1] for t in range(1, SLOTS)]
    last = [jnp.where(same[t], -1, owner[t]) for t in range(SLOTS - 1)] + [owner[SLOTS - 1]]
    for r in range(REQUESTS):
        at = jnp.int32(0)
        for t in range(SLOTS):
            at = jnp.where(last[t] == r, t, at)
        place[r] = at
    column = [
        jnp.where(r < 0, -128, ((r >> 1) & 1) * 64 + (r & 1) * 8 + (r >> 2)) for r in last]

    def lanes(p):
        return lax.broadcasted_iota(jnp.int32, (ROWS[p], 128), 1)

    def attend(p):
        lane = lanes(p)
        tops = []
        for t in range(SLOTS):
            r = owner[t]
            q = gq[p][(r >> 1) & 1, r >> 2, r & 1]
            score = jnp.concatenate(
                [lax.dot_general(
                    q[GROUP * g:GROUP * (g + 1)], kbuf[p][t, :, HEAD * g:HEAD * (g + 1)],
                    (((1,), (1,)), ((), ())), preferred_element_type=jnp.float32)
                 for g in range(WIDTHS[p])], axis=0) * SCALE
            score = jnp.where(token < limit[t], score, -jnp.inf)
            scores[p][t] = score
            tops.append(jnp.max(
                jnp.maximum(score[:, :128], score[:, 128:]), axis=1, keepdims=True))
        for t in range(1, SLOTS):
            tops[t] = jnp.maximum(jnp.where(same[t - 1], tops[t - 1], -jnp.inf), tops[t])
        for t in range(SLOTS - 2, -1, -1):
            tops[t] = jnp.where(same[t], tops[t + 1], tops[t])
        mix, total = None, None
        meta = jnp.where((lane & 63) < 16, NONE, 0.0)
        for t in range(SLOTS):
            weight = jnp.exp(scores[p][t] - tops[t]).astype(jnp.bfloat16)
            part = jnp.concatenate(
                [jnp.dot(
                    weight[GROUP * g:GROUP * (g + 1)], vbuf[p][t, :, HEAD * g:HEAD * (g + 1)],
                    preferred_element_type=jnp.float32)
                 for g in range(WIDTHS[p])], axis=0)
            wide = weight.astype(jnp.float32)
            count = jnp.sum(wide[:, :128] + wide[:, 128:], axis=1, keepdims=True)
            mix = part if t == 0 else jnp.where(same[t - 1], mix, 0.0) + part
            total = count if t == 0 else jnp.where(same[t - 1], total, 0.0) + count
            sums_of[p][t] = mix
            meta = jnp.where(lane == column[t], tops[t], meta)
            meta = jnp.where(lane == column[t] + 16, total, meta)
        meta_own[p][...] = meta
        pltpu.make_async_remote_copy(
            src_ref=meta_own[p], dst_ref=twin_meta[p],
            send_sem=twin_m_send_sem.at[p], recv_sem=twin_m_sem.at[p],
            device_id=(section, twin), device_id_type=MESH).start()
        for c in range(CHIPS):
            for i in range(2):
                twin_send[p][c, i] = sums_of[p][place[4 * c + 2 * (1 - core) + i]].astype(jnp.bfloat16)
        pltpu.make_async_remote_copy(
            src_ref=twin_send[p], dst_ref=twin_x[p],
            send_sem=twin_x_send_sem.at[p], recv_sem=twin_x_sem.at[p],
            device_id=(section, twin), device_id_type=MESH).start()

    def join_cores(p):
        lane, rows = lanes(p), ROWS[p]
        landed(twin_meta[p], twin_m_sem.at[p])
        here = pltpu.roll(meta_own[p][...], 64 * core, 1)
        there = pltpu.roll(twin_meta[p][...], 64 * core, 1)
        peak = jnp.maximum(here, there)
        by_here, by_there = jnp.exp(here - peak), jnp.exp(there - peak)
        total = by_here * pltpu.roll(here, 112, 1) + by_there * pltpu.roll(there, 112, 1)
        meta = jnp.where(lane < 16, peak, jnp.where(lane < 32, pltpu.roll(total, 16, 1), 0.0))
        turned = jnp.concatenate([meta, jnp.zeros((128 - rows, 128), jnp.float32)], axis=0).T
        table = widen(jnp.concatenate(
            [turned[CHIPS * i:CHIPS * (i + 1), :rows] for i in range(4)], axis=1))
        for c in range(CHIPS):
            m_send[p][c] = table[c:c + 1]
        if p >= TWICE:
            for to in others + [chip]:
                pltpu.make_async_remote_copy(
                    src_ref=m_send[p].at[to], dst_ref=ym_got[p - TWICE].at[chip],
                    send_sem=ym_send_sem.at[p - TWICE], recv_sem=ym_sem.at[p - TWICE],
                    device_id=(after, 2 * to + core), device_id_type=MESH).start()
        for to in others:
            pltpu.make_async_remote_copy(
                src_ref=m_send[p].at[to], dst_ref=mr[p].at[chip],
                send_sem=m_send_sem.at[p], recv_sem=m_sem.at[p],
                device_id=(section, 2 * to + core), device_id_type=MESH).start()
        pltpu.make_async_copy(m_send[p].at[chip], mr[p].at[chip], m_sem.at[p]).start()
        landed(twin_x[p], twin_x_sem.at[p])
        for c in range(CHIPS):
            for i in range(2):
                at = 8 * i + c
                own = sums_of[p][place[4 * c + 2 * core + i]]
                other = twin_x[p][c, i].astype(jnp.float32)
                x_send[p][c, i] = (
                    by_here[:, at:at + 1] * own + by_there[:, at:at + 1] * other).astype(jnp.bfloat16)
        if p >= TWICE:
            for to in others + [chip]:
                pltpu.make_async_remote_copy(
                    src_ref=x_send[p].at[to], dst_ref=y_got[p - TWICE].at[chip],
                    send_sem=y_send_sem.at[p - TWICE], recv_sem=y_sem.at[p - TWICE],
                    device_id=(after, 2 * to + core), device_id_type=MESH).start()
        for to in others:
            pltpu.make_async_remote_copy(
                src_ref=x_send[p].at[to], dst_ref=xr[p].at[chip],
                send_sem=x_send_sem.at[p], recv_sem=x_sem.at[p],
                device_id=(section, 2 * to + core), device_id_type=MESH).start()
        pltpu.make_async_copy(x_send[p].at[chip], xr[p].at[chip], x_sem.at[p]).start()

    def join_chips(p, got, got_sem, lines, lines_sem, finish):
        lane, rows = lanes(p), ROWS[p]
        landed(lines, lines_sem)
        table = jnp.concatenate([lines[c] for c in range(CHIPS)], axis=0)
        kinds = jnp.concatenate([table[:, rows * i:rows * (i + 1)] for i in range(4)], axis=0)
        kinds = jnp.concatenate([kinds, jnp.zeros((32, 128 - rows), jnp.float32)], axis=1)
        meta = jnp.concatenate([kinds, jnp.zeros((128 - 32, 128), jnp.float32)], axis=0).T[:rows]
        totals = pltpu.roll(meta, 112, 1)
        landed(got, got_sem)
        for i in range(2):
            used = (lane >> 3) == i
            peaks = jnp.where(used, meta, NONE)
            part = jnp.exp(peaks - jnp.max(peaks, axis=1, keepdims=True))
            whole = jnp.sum(jnp.where(used, part * totals, 0.0), axis=1, keepdims=True)
            part = part / whole
            mix = None
            for c in range(CHIPS):
                at = 8 * i + c
                term = part[:, at:at + 1] * got[c, i].astype(jnp.float32)
                mix = term if mix is None else mix + term
            finish(i, mix.astype(jnp.bfloat16))

    def finish_here(p):
        heads = pl.ds(GROUP * FIRST[p], ROWS[p])

        def finish(i, attended):
            att_ref[i, heads, :] = attended
            if p < TWICE:
                hand_send[p][i] = (
                    res_f32[i, heads, :] + attended.astype(jnp.float32)).astype(jnp.bfloat16)

        join_chips(p, xr[p], x_sem.at[p], mr[p], m_sem.at[p], finish)
        if p < TWICE:
            pltpu.make_async_remote_copy(
                src_ref=hand_send[p], dst_ref=nxt_ref.at[:, heads, :],
                send_sem=hand_send_sem.at[p], recv_sem=hand_sem,
                device_id=(after, me), device_id_type=MESH).start()

    def finish_before(p):
        heads = pl.ds(GROUP * FIRST[p], ROWS[p])
        rows = pl.ds(GROUP * (FIRST[p] - FIRST[TWICE]), ROWS[p])
        k = p - TWICE

        def finish(i, attended):
            nxt_ref[i, heads, :] = (
                prev_res[i, rows, :].astype(jnp.float32) + attended.astype(jnp.float32)).astype(jnp.bfloat16)

        join_chips(p, y_got[k], y_sem.at[k], ym_got[k], ym_sem.at[k], finish)

    passed = [pass_queries(0), pass_queries(1)]
    for p in range(PHASES):
        passed[p].wait_recv()
        loads[2 * p].wait()
        loads[2 * p + 1].wait()
        attend(p)
        if p + 2 < PHASES:
            passed.append(pass_queries(p + 2))
        if p > 0:
            join_cores(p - 1)
    for p in range(EARLY):
        finish_here(p)
    join_cores(LAST)
    for p in range(EARLY, PHASES):
        finish_here(p)
        if p == TWICE - 1:
            pass_residual.wait()
        if p >= TWICE:
            finish_before(p)

    for p in range(PHASES):
        landed(gq[p].at[0, pl.ds(0, 7)], gq_send_sem.at[p])
        landed(gq[p].at[0], gq_send_sem.at[p])
        landed(x_send[p].at[pl.ds(0, 7)], x_send_sem.at[p])
        landed(m_send[p].at[pl.ds(0, 7)], m_send_sem.at[p])
        landed(twin_send[p], twin_x_send_sem.at[p])
        landed(meta_own[p], twin_m_send_sem.at[p])
        if p < TWICE:
            landed(hand_send[p], hand_send_sem.at[p])
    for p in range(TWICE, PHASES):
        landed(x_send[p], y_send_sem.at[p - TWICE])
        landed(m_send[p], ym_send_sem.at[p - TWICE])
    landed(nxt_ref.at[:, pl.ds(0, GROUP * FIRST[TWICE]), :], hand_sem)


def local(
    queries, residual, key_tile_store, value_tile_store, lengths, tile_request, tile_position
):
    any_spec = pl.BlockSpec(memory_space=pl.ANY)
    vmem_spec = pl.BlockSpec(memory_space=pltpu.VMEM)
    dma = pltpu.SemaphoreType.DMA
    bf16, f32 = jnp.bfloat16, jnp.float32
    def each(dtype, shape):
        return [pltpu.VMEM(shape(w, r), dtype) for w, r in zip(WIDTHS, ROWS, strict=True)]

    sums = (CHIPS, 2)
    scratch = (
        [pltpu.SMEM(a.shape, jnp.int32) for a in (lengths, tile_request, tile_position)]
        + [pltpu.VMEM((2, HEADS * HEAD), bf16)] * 2
        + [pltpu.VMEM((2, HEADS, HEAD), f32)] * 2
        + [pltpu.VMEM((2, HEADS - GROUP * FIRST[TWICE], HEAD), bf16)] * 2
        + [pltpu.SMEM((REQUESTS,), jnp.int32)]
        + each(bf16, lambda w, r: (2, r, HEAD))
        + each(bf16, lambda w, r: (2, *sums, r, HEAD))
        + each(bf16, lambda w, r: (SLOTS, TILE, w * HEAD)) * 2
        + each(f32, lambda w, r: (SLOTS, r, TILE))
        + each(f32, lambda w, r: (SLOTS, r, HEAD))
        + each(f32, lambda w, r: (r, 128)) * 2
        + each(bf16, lambda w, r: (*sums, r, HEAD)) * 2
        + each(bf16, lambda w, r: (*sums, r, HEAD)) * 2
        + each(f32, lambda w, r: (CHIPS, 1, 128)) * 2
        + each(bf16, lambda w, r: (2, r, HEAD))
        + each(bf16, lambda w, r: (*sums, r, HEAD))[TWICE:]
        + each(f32, lambda w, r: (CHIPS, 1, 128))[TWICE:]
        + [dma, dma, dma((3,)), dma((PHASES, 2))] + [dma((PHASES,))] * 12 + [dma] * 3 + [dma((PHASES - TWICE,))] * 4
    )
    attended, handed = pl.pallas_call(
        kernel,
        out_shape=(pltpu.VMEM((2, HEADS, HEAD), bf16),) * 2,
        in_specs=[any_spec] * 7,
        out_specs=[vmem_spec] * 2,
        scratch_shapes=scratch,
        compiler_params=pltpu.CompilerParams(
            collective_id=0, has_side_effects=True, vmem_limit_bytes=60 * 1024 * 1024),
    )(queries, residual, key_tile_store, value_tile_store, lengths, tile_request, tile_position)
    return attended.reshape(queries.shape), handed.reshape(queries.shape)


def solution(mesh):
    in_specs = (
        P(("section", "peer"), None),
        P(("section", "peer"), None),
        P("section", "peer", None, None),
        P("section", "peer", None, None),
        P("section", None),
        P("section", "peer"),
        P("section", "peer"),
    )
    out_specs = (P(("section", "peer"), None), P(("section", "peer"), None))
    return jax.shard_map(local, mesh=mesh, in_specs=in_specs, out_specs=out_specs, check_vma=False)
```

```python
import jax
import jax.numpy as jnp
from jax import lax
from jax.experimental import pallas as pl
from jax.experimental.pallas import tpu as pltpu
from jax.sharding import PartitionSpec as P

PEERS = 16
CHIPS = 8
SECTIONS = 8
SLOTS = 16
TILE = 256
HEADS = 128
HEAD = 128
REQUESTS = 32
GROUP = 16
WIDTHS = (2, 2, 2, 2)
PHASES = len(WIDTHS)
TWICE = 3
EARLY = 1
LAST = PHASES - 1
FIRST = [sum(WIDTHS[:p]) for p in range(PHASES)]
ROWS = [GROUP * w for w in WIDTHS]
SCALE = HEAD ** (-0.5)
NONE = -1e30
STEPS = ((1, 2), (1, 1), (1, 3), (1, 0), (0, 2), (0, 1), (0, 3))
MESH = pl.DeviceIdType.MESH


def widen(block):
    rest = 128 - block.shape[1]
    if not rest:
        return block
    return jnp.concatenate([block, jnp.zeros((block.shape[0], rest), block.dtype)], axis=1)


def landed(ref, sem):
    pltpu.make_async_copy(ref, ref, sem).wait()


def kernel(
    q_hbm, res_hbm, k_hbm, v_hbm, len_hbm, req_hbm, pos_hbm,
    att_ref, nxt_ref,
    len_ref, req_ref, pos_ref, q_in, res_in, q_f32, res_f32, res_send, prev_res, place, *rest,
):
    q_send, gq, kbuf, vbuf, scores, sums_of, meta_own, twin_meta, twin_send, twin_x, x_send, xr, m_send, mr, hand_send = (
        rest[i * PHASES:(i + 1) * PHASES] for i in range(15))
    (
        q_sem, res_sem, plan_sem, kv_sem, gq_send_sem, gq_recv_sem, gq_twin_sem,
        twin_x_send_sem, twin_x_sem, twin_m_send_sem, twin_m_sem,
        x_send_sem, x_sem, m_send_sem, m_sem, hand_send_sem, hand_sem,
        res_send_sem, prev_res_sem, y_send_sem, y_sem, ym_send_sem, ym_sem,
    ) = rest[15 * PHASES + 2 * (PHASES - TWICE):]
    y_got = rest[15 * PHASES:][:PHASES - TWICE]
    ym_got = rest[15 * PHASES:][PHASES - TWICE:2 * (PHASES - TWICE)]
    me = lax.axis_index("peer")
    section = lax.axis_index("section")
    core, chip = lax.rem(me, 2), me // 2
    y, z = chip // 4, lax.rem(chip, 4)
    others = [lax.rem(y + dy, 2) * 4 + lax.rem(z + dz, 4) for dy, dz in STEPS]
    twin = me + 1 - 2 * core
    after = lax.rem(section + 1, SECTIONS)
    before = lax.rem(section + SECTIONS - 1, SECTIONS)

    barrier = pltpu.get_barrier_semaphore()

    for to in others:
        pl.semaphore_signal(
            barrier, inc=1, device_id=(section, 2 * to + core), device_id_type=MESH)
    pl.semaphore_signal(barrier, inc=1, device_id=(before, me), device_id_type=MESH)
    pl.semaphore_signal(barrier, inc=1, device_id=(section, twin), device_id_type=MESH)

    q_copy = pltpu.make_async_copy(q_hbm, q_in, q_sem)
    q_copy.start()
    res_copy = pltpu.make_async_copy(res_hbm, res_in, res_sem)
    res_copy.start()
    plan = []
    for i, (src, dst) in enumerate(((len_hbm, len_ref), (req_hbm, req_ref), (pos_hbm, pos_ref))):
        plan.append(pltpu.make_async_copy(src, dst, plan_sem.at[i]))
        plan[i].start()
    def spread(rows, out):
        for h in range(HEADS):
            piece = rows[:, h * HEAD:(h + 1) * HEAD].astype(jnp.float32)
            out[0, h:h + 1, :] = piece[0:1]
            out[1, h:h + 1, :] = piece[1:2]

    q_copy.wait()
    spread(q_in, q_f32)
    for p in range(PHASES):
        q_send[p][...] = q_f32[:, GROUP * FIRST[p]:GROUP * FIRST[p] + ROWS[p], :].astype(jnp.bfloat16)

    pl.semaphore_wait(barrier, CHIPS + 1)

    for p in range(PHASES):
        for to in others:
            pltpu.make_async_remote_copy(
                src_ref=q_send[p], dst_ref=gq[p].at[core, chip],
                send_sem=gq_send_sem.at[p], recv_sem=gq_recv_sem.at[p],
                device_id=(section, 2 * to + core), device_id_type=MESH).start()
        pltpu.make_async_copy(q_send[p], gq[p].at[core, chip], gq_recv_sem.at[p]).start()
    loads = []
    for p in range(PHASES):
        cols = pl.ds(FIRST[p] * HEAD, WIDTHS[p] * HEAD)
        for i, (src, dst) in enumerate(((k_hbm, kbuf), (v_hbm, vbuf))):
            load = pltpu.make_async_copy(
                src.at[0, :, :, cols], dst[p], kv_sem.at[p, i])
            load.start()
            loads.append(load)

    def pass_queries(p):
        landed(gq[p].at[core], gq_recv_sem.at[p])
        copy = pltpu.make_async_remote_copy(
            src_ref=gq[p].at[core], dst_ref=gq[p].at[core],
            send_sem=gq_send_sem.at[p], recv_sem=gq_twin_sem.at[p],
            device_id=(section, twin), device_id_type=MESH)
        copy.start()
        return copy

    res_copy.wait()
    spread(res_in, res_f32)
    res_send[...] = res_f32[:, GROUP * FIRST[TWICE]:, :].astype(jnp.bfloat16)
    pass_residual = pltpu.make_async_remote_copy(
        src_ref=res_send, dst_ref=prev_res, send_sem=res_send_sem, recv_sem=prev_res_sem,
        device_id=(after, me), device_id_type=MESH)
    pass_residual.start()
    for copy in plan:
        copy.wait()

    token = lax.broadcasted_iota(jnp.int32, (1, TILE), 1)
    owner = [req_ref[0, t] for t in range(SLOTS)]
    limit = [len_ref[0, owner[t]] - pos_ref[0, t] * TILE for t in range(SLOTS)]
    same = [owner[t] == owner[t - 1] for t in range(1, SLOTS)]
    last = [jnp.where(same[t], -1, owner[t]) for t in range(SLOTS - 1)] + [owner[SLOTS - 1]]
    for r in range(REQUESTS):
        at = jnp.int32(0)
        for t in range(SLOTS):
            at = jnp.where(last[t] == r, t, at)
        place[r] = at
    column = [
        jnp.where(r < 0, -128, ((r >> 1) & 1) * 64 + (r & 1) * 8 + (r >> 2)) for r in last]

    def lanes(p):
        return lax.broadcasted_iota(jnp.int32, (ROWS[p], 128), 1)

    def attend(p):
        lane = lanes(p)
        tops = []
        for t in range(SLOTS):
            r = owner[t]
            q = gq[p][(r >> 1) & 1, r >> 2, r & 1]
            score = jnp.concatenate(
                [lax.dot_general(
                    q[GROUP * g:GROUP * (g + 1)], kbuf[p][t, :, HEAD * g:HEAD * (g + 1)],
                    (((1,), (1,)), ((), ())), preferred_element_type=jnp.float32)
                 for g in range(WIDTHS[p])], axis=0) * SCALE
            score = jnp.where(token < limit[t], score, -jnp.inf)
            scores[p][t] = score
            tops.append(jnp.max(
                jnp.maximum(score[:, :128], score[:, 128:]), axis=1, keepdims=True))
        for t in range(1, SLOTS):
            tops[t] = jnp.maximum(jnp.where(same[t - 1], tops[t - 1], -jnp.inf), tops[t])
        for t in range(SLOTS - 2, -1, -1):
            tops[t] = jnp.where(same[t], tops[t + 1], tops[t])
        mix, total = None, None
        meta = jnp.where((lane & 63) < 16, NONE, 0.0)
        for t in range(SLOTS):
            weight = jnp.exp(scores[p][t] - tops[t]).astype(jnp.bfloat16)
            part = jnp.concatenate(
                [jnp.dot(
                    weight[GROUP * g:GROUP * (g + 1)], vbuf[p][t, :, HEAD * g:HEAD * (g + 1)],
                    preferred_element_type=jnp.float32)
                 for g in range(WIDTHS[p])], axis=0)
            wide = weight.astype(jnp.float32)
            count = jnp.sum(wide[:, :128] + wide[:, 128:], axis=1, keepdims=True)
            mix = part if t == 0 else jnp.where(same[t - 1], mix, 0.0) + part
            total = count if t == 0 else jnp.where(same[t - 1], total, 0.0) + count
            sums_of[p][t] = mix
            meta = jnp.where(lane == column[t], tops[t], meta)
            meta = jnp.where(lane == column[t] + 16, total, meta)
        meta_own[p][...] = meta
        pltpu.make_async_remote_copy(
            src_ref=meta_own[p], dst_ref=twin_meta[p],
            send_sem=twin_m_send_sem.at[p], recv_sem=twin_m_sem.at[p],
            device_id=(section, twin), device_id_type=MESH).start()
        for c in range(CHIPS):
            for i in range(2):
                twin_send[p][c, i] = sums_of[p][place[4 * c + 2 * (1 - core) + i]].astype(jnp.bfloat16)
        pltpu.make_async_remote_copy(
            src_ref=twin_send[p], dst_ref=twin_x[p],
            send_sem=twin_x_send_sem.at[p], recv_sem=twin_x_sem.at[p],
            device_id=(section, twin), device_id_type=MESH).start()

    def join_cores(p, meanwhile=()):
        lane, rows = lanes(p), ROWS[p]
        landed(twin_meta[p], twin_m_sem.at[p])
        here = pltpu.roll(meta_own[p][...], 64 * core, 1)
        there = pltpu.roll(twin_meta[p][...], 64 * core, 1)
        peak = jnp.maximum(here, there)
        by_here, by_there = jnp.exp(here - peak), jnp.exp(there - peak)
        total = by_here * pltpu.roll(here, 112, 1) + by_there * pltpu.roll(there, 112, 1)
        meta = jnp.where(lane < 16, peak, jnp.where(lane < 32, pltpu.roll(total, 16, 1), 0.0))
        turned = jnp.concatenate([meta, jnp.zeros((128 - rows, 128), jnp.float32)], axis=0).T
        table = widen(jnp.concatenate(
            [turned[CHIPS * i:CHIPS * (i + 1), :rows] for i in range(4)], axis=1))
        for c in range(CHIPS):
            m_send[p][c] = table[c:c + 1]
        if p >= TWICE:
            for to in others + [chip]:
                pltpu.make_async_remote_copy(
                    src_ref=m_send[p].at[to], dst_ref=ym_got[p - TWICE].at[chip],
                    send_sem=ym_send_sem.at[p - TWICE], recv_sem=ym_sem.at[p - TWICE],
                    device_id=(after, 2 * to + core), device_id_type=MESH).start()
        for to in others:
            pltpu.make_async_remote_copy(
                src_ref=m_send[p].at[to], dst_ref=mr[p].at[chip],
                send_sem=m_send_sem.at[p], recv_sem=m_sem.at[p],
                device_id=(section, 2 * to + core), device_id_type=MESH).start()
        pltpu.make_async_copy(m_send[p].at[chip], mr[p].at[chip], m_sem.at[p]).start()
        for earlier in meanwhile:
            finish_here(earlier)
        landed(twin_x[p], twin_x_sem.at[p])
        for c in range(CHIPS):
            for i in range(2):
                at = 8 * i + c
                own = sums_of[p][place[4 * c + 2 * core + i]]
                other = twin_x[p][c, i].astype(jnp.float32)
                x_send[p][c, i] = (
                    by_here[:, at:at + 1] * own + by_there[:, at:at + 1] * other).astype(jnp.bfloat16)
        if p >= TWICE:
            for to in others + [chip]:
                pltpu.make_async_remote_copy(
                    src_ref=x_send[p].at[to], dst_ref=y_got[p - TWICE].at[chip],
                    send_sem=y_send_sem.at[p - TWICE], recv_sem=y_sem.at[p - TWICE],
                    device_id=(after, 2 * to + core), device_id_type=MESH).start()
        for to in others:
            pltpu.make_async_remote_copy(
                src_ref=x_send[p].at[to], dst_ref=xr[p].at[chip],
                send_sem=x_send_sem.at[p], recv_sem=x_sem.at[p],
                device_id=(section, 2 * to + core), device_id_type=MESH).start()
        pltpu.make_async_copy(x_send[p].at[chip], xr[p].at[chip], x_sem.at[p]).start()

    def join_chips(p, got, got_sem, lines, lines_sem, finish):
        lane, rows = lanes(p), ROWS[p]
        landed(lines, lines_sem)
        table = jnp.concatenate([lines[c] for c in range(CHIPS)], axis=0)
        kinds = jnp.concatenate([table[:, rows * i:rows * (i + 1)] for i in range(4)], axis=0)
        kinds = jnp.concatenate([kinds, jnp.zeros((32, 128 - rows), jnp.float32)], axis=1)
        meta = jnp.concatenate([kinds, jnp.zeros((128 - 32, 128), jnp.float32)], axis=0).T[:rows]
        totals = pltpu.roll(meta, 112, 1)
        landed(got, got_sem)
        for i in range(2):
            used = (lane >> 3) == i
            peaks = jnp.where(used, meta, NONE)
            part = jnp.exp(peaks - jnp.max(peaks, axis=1, keepdims=True))
            whole = jnp.sum(jnp.where(used, part * totals, 0.0), axis=1, keepdims=True)
            part = part / whole
            mix = None
            for c in range(CHIPS):
                at = 8 * i + c
                term = part[:, at:at + 1] * got[c, i].astype(jnp.float32)
                mix = term if mix is None else mix + term
            finish(i, mix.astype(jnp.bfloat16))

    def finish_here(p):
        heads = pl.ds(GROUP * FIRST[p], ROWS[p])

        def finish(i, attended):
            att_ref[i, heads, :] = attended
            if p < TWICE:
                hand_send[p][i] = (
                    res_f32[i, heads, :] + attended.astype(jnp.float32)).astype(jnp.bfloat16)

        join_chips(p, xr[p], x_sem.at[p], mr[p], m_sem.at[p], finish)
        if p < TWICE:
            pltpu.make_async_remote_copy(
                src_ref=hand_send[p], dst_ref=nxt_ref.at[:, heads, :],
                send_sem=hand_send_sem.at[p], recv_sem=hand_sem,
                device_id=(after, me), device_id_type=MESH).start()

    def finish_before(p):
        heads = pl.ds(GROUP * FIRST[p], ROWS[p])
        rows = pl.ds(GROUP * (FIRST[p] - FIRST[TWICE]), ROWS[p])
        k = p - TWICE

        def finish(i, attended):
            nxt_ref[i, heads, :] = (
                prev_res[i, rows, :].astype(jnp.float32) + attended.astype(jnp.float32)).astype(jnp.bfloat16)

        join_chips(p, y_got[k], y_sem.at[k], ym_got[k], ym_sem.at[k], finish)

    passed = [pass_queries(0), pass_queries(1)]
    for p in range(PHASES):
        passed[p].wait_recv()
        loads[2 * p].wait()
        loads[2 * p + 1].wait()
        attend(p)
        if p + 2 < PHASES:
            passed.append(pass_queries(p + 2))
        if p > 0:
            join_cores(p - 1)
    join_cores(LAST, range(EARLY))
    for p in range(EARLY, PHASES):
        finish_here(p)
        if p == TWICE - 1:
            pass_residual.wait()
        if p >= TWICE:
            finish_before(p)

    for p in range(PHASES):
        landed(gq[p].at[0, pl.ds(0, 7)], gq_send_sem.at[p])
        landed(gq[p].at[0], gq_send_sem.at[p])
        landed(x_send[p].at[pl.ds(0, 7)], x_send_sem.at[p])
        landed(m_send[p].at[pl.ds(0, 7)], m_send_sem.at[p])
        landed(twin_send[p], twin_x_send_sem.at[p])
        landed(meta_own[p], twin_m_send_sem.at[p])
        if p < TWICE:
            landed(hand_send[p], hand_send_sem.at[p])
    for p in range(TWICE, PHASES):
        landed(x_send[p], y_send_sem.at[p - TWICE])
        landed(m_send[p], ym_send_sem.at[p - TWICE])
    landed(nxt_ref.at[:, pl.ds(0, GROUP * FIRST[TWICE]), :], hand_sem)


def local(
    queries, residual, key_tile_store, value_tile_store, lengths, tile_request, tile_position
):
    any_spec = pl.BlockSpec(memory_space=pl.ANY)
    vmem_spec = pl.BlockSpec(memory_space=pltpu.VMEM)
    dma = pltpu.SemaphoreType.DMA
    bf16, f32 = jnp.bfloat16, jnp.float32
    def each(dtype, shape):
        return [pltpu.VMEM(shape(w, r), dtype) for w, r in zip(WIDTHS, ROWS, strict=True)]

    sums = (CHIPS, 2)
    scratch = (
        [pltpu.SMEM(a.shape, jnp.int32) for a in (lengths, tile_request, tile_position)]
        + [pltpu.VMEM((2, HEADS * HEAD), bf16)] * 2
        + [pltpu.VMEM((2, HEADS, HEAD), f32)] * 2
        + [pltpu.VMEM((2, HEADS - GROUP * FIRST[TWICE], HEAD), bf16)] * 2
        + [pltpu.SMEM((REQUESTS,), jnp.int32)]
        + each(bf16, lambda w, r: (2, r, HEAD))
        + each(bf16, lambda w, r: (2, *sums, r, HEAD))
        + each(bf16, lambda w, r: (SLOTS, TILE, w * HEAD)) * 2
        + each(f32, lambda w, r: (SLOTS, r, TILE))
        + each(f32, lambda w, r: (SLOTS, r, HEAD))
        + each(f32, lambda w, r: (r, 128)) * 2
        + each(bf16, lambda w, r: (*sums, r, HEAD)) * 2
        + each(bf16, lambda w, r: (*sums, r, HEAD)) * 2
        + each(f32, lambda w, r: (CHIPS, 1, 128)) * 2
        + each(bf16, lambda w, r: (2, r, HEAD))
        + each(bf16, lambda w, r: (*sums, r, HEAD))[TWICE:]
        + each(f32, lambda w, r: (CHIPS, 1, 128))[TWICE:]
        + [dma, dma, dma((3,)), dma((PHASES, 2))] + [dma((PHASES,))] * 12 + [dma] * 3 + [dma((PHASES - TWICE,))] * 4
    )
    attended, handed = pl.pallas_call(
        kernel,
        out_shape=(pltpu.VMEM((2, HEADS, HEAD), bf16),) * 2,
        in_specs=[any_spec] * 7,
        out_specs=[vmem_spec] * 2,
        scratch_shapes=scratch,
        compiler_params=pltpu.CompilerParams(
            collective_id=0, has_side_effects=True, vmem_limit_bytes=60 * 1024 * 1024),
    )(queries, residual, key_tile_store, value_tile_store, lengths, tile_request, tile_position)
    return attended.reshape(queries.shape), handed.reshape(queries.shape)


def solution(mesh):
    in_specs = (
        P(("section", "peer"), None),
        P(("section", "peer"), None),
        P("section", "peer", None, None),
        P("section", "peer", None, None),
        P("section", None),
        P("section", "peer"),
        P("section", "peer"),
    )
    out_specs = (P(("section", "peer"), None), P(("section", "peer"), None))
    return jax.shard_map(local, mesh=mesh, in_specs=in_specs, out_specs=out_specs, check_vma=False)
```
